32 devices in a mesh: groups: 2 (over y), frame: 4 (over z), panel: 2 (over x), sub: 2 (over core).
Axes of the slice: x: 2, y: 2, z: 4, core: 2. Of those that a mesh axis runs over, the one named last changes fastest.
Arguments:
- frames: bfloat16 [2048, 65536], P(('groups', 'frame'), ('panel', 'sub')), parts along dimension 0, may hold values from -16 to 16
- slices: float32 [32, 65536], P(('groups', 'frame'), ('panel', 'sub')), parts along dimension 0, may hold values from -8 to 8
- log_prior: float32 [4096], replicated, may hold values from -2 to 2
- orient: int32 [32], P('groups'), parts along dimension 0, may hold values from 0 to 4095
Outputs:
- new_slices: float32 [32, 65536], P(('groups', 'frame'), ('panel', 'sub')), parts along dimension 0
The draws below stay inside these ranges and needn't reach their ends.
There are 2 independent parts, one for each index of `groups`. The reference program is written for one: setup_inputs(seed, part) draws one part's arguments, and reference() takes and returns one part's arrays. A program takes and returns all parts, laid end to end along the dimension named above; an argument that names none is the same for every part. Nothing has to cross between parts.
All inputs are finite; a program needn't handle non-finite values.
Results may differ from the reference program's by a relative error of at most 0.022.
The reference program's roundings to bfloat16 on the way (of `rounded` and `weights`) count: a program that leaves them out, or rounds other values in their place, can miss the bound.
Values may be sent and summed in bfloat16 or wider, within the bound.
No kernel may reach another device: no remote copies, remote signals or barrier semaphores. Data moves between devices by JAX's collectives and lax.ppermute only.
A program may use at most 64 MiB of HBM per device.

```python
import math
import jax
import jax.numpy as jnp
from jax import lax

PIX = 65536
FRAMES_DEV = 256
NORIENT = 4096
ITERS = 2
FRAMES = 1024
SLICES = 16
N_FRAME = 4


def pixel_scale(key):
    lower = 0.5
    upper = 2.0
    unit = jax.random.uniform(jax.random.fold_in(key, 31), (PIX,), jnp.float32)
    return lower * jnp.exp(unit * math.log(upper / lower))


def unit_entries(key, shape):
    return jax.random.truncated_normal(key, -4.0, 4.0, shape, jnp.float32)


def slice_values(key):
    scale = pixel_scale(key)
    return unit_entries(jax.random.fold_in(key, 32), (SLICES, PIX)) * scale[None, :]


def draw_slices(key, part):
    return slice_values(key)


def draw_frames(key, part):
    source = slice_values(key)
    scale = pixel_scale(key)
    chosen = jax.random.randint(jax.random.fold_in(key, 33), (FRAMES,), 0, SLICES)
    level = jax.random.uniform(jax.random.fold_in(key, 34), (FRAMES,), jnp.float32)
    signal = jnp.exp(level * math.log(4.0)) / math.sqrt(PIX)
    noise = unit_entries(jax.random.fold_in(key, 35), (FRAMES, PIX)) * scale[None, :]
    picked = source[chosen]
    result = signal[:, None] * picked + noise
    return result.astype(jnp.bfloat16)


def set_ends(drawn, rng, least, largest):
    spot = [jax.random.randint(jax.random.fold_in(rng, axis), (), 0, length) for axis, length in enumerate(drawn.shape)]
    widest = drawn.shape.index(max(drawn.shape))
    beside = spot[:widest] + [(spot[widest] + 1) % drawn.shape[widest]] + spot[widest + 1:]
    return drawn.at[tuple(spot)].set(least).at[tuple(beside)].set(largest)


def setup_inputs(seed: int = 0, part: int = 0) -> dict:
    keys = jax.random.split(jax.random.key(seed), 5)
    part_keys = jax.random.split(jax.random.fold_in(keys[4], part), 5)
    return {
        "frames": draw_frames(jax.random.fold_in(jax.random.fold_in(keys[4], part), 71), part),
        "slices": draw_slices(jax.random.fold_in(jax.random.fold_in(keys[4], part), 71), part),
        "log_prior": jnp.clip(jax.random.uniform(keys[2], (NORIENT,), jnp.float32, -2.0, 2.0), -2.0, 2.0),
        "orient": set_ends(jax.random.randint(part_keys[3], (SLICES,), 0, NORIENT), jax.random.fold_in(part_keys[3], 1), 0, NORIENT - 1).astype(jnp.int32),
    }


def reference(frames, slices, log_prior, orient):
    prior = log_prior[orient]
    temper = 3.0 / math.sqrt(PIX)
    blocks = frames.reshape(N_FRAME, FRAMES_DEV, PIX)
    current = slices
    for step in range(ITERS):
        rounded = current.astype(jnp.bfloat16)
        wide = rounded.astype(jnp.float32)
        norms = lax.optimization_barrier(jnp.sum(wide * wide, axis=1))
        raw = jnp.dot(frames, rounded.T, preferred_element_type=jnp.float32) - 0.5 * norms[None, :]
        scores = temper * raw + prior[None, :]
        weights = jax.nn.softmax(scores, axis=1).astype(jnp.bfloat16)
        counts = lax.optimization_barrier(jnp.sum(weights.astype(jnp.float32), axis=0))
        weight_blocks = weights.reshape(N_FRAME, FRAMES_DEV, SLICES)

        def add_block(total, pair):
            block_w, block_f = pair
            term = jnp.dot(block_w.T, block_f, preferred_element_type=jnp.float32)
            term = lax.optimization_barrier(term.astype(jnp.bfloat16))
            return (total + term.astype(jnp.float32), None)
        totals, _ = lax.scan(add_block, jnp.zeros((SLICES, PIX), jnp.float32), (weight_blocks, blocks))
        current = (totals + wide) / (counts + 1.0)[:, None]
    return current
```

```python
import functools
import math

import jax
import jax.numpy as jnp
from jax import lax
from jax.experimental import pallas as pl
from jax.experimental.pallas import tpu as pltpu
from jax.sharding import PartitionSpec as P

PIX = 65536
ITERS = 2
TAIL = 128
DIRECT = 8
VMEM_BYTES = 32 * 1024 * 1024


def tree_sum(terms):
    while len(terms) > 1:
        terms = [a + b for a, b in zip(terms[::2], terms[1::2])] + terms[len(terms) & ~1 :]
    return terms[0]


def spread(block, axis, size, sign):
    return [
        lax.ppermute(block[k] if isinstance(block, list) else block, axis, [(i, (i + sign * k) % size) for i in range(size)])
        for k in range(1, size)
    ]


def exchange_all(part, axes, size):
    if size & (size - 1):
        return [lax.psum(part, axes)]
    return [part] + [lax.ppermute(part, axes, [(i, i ^ k) for i in range(size)]) for k in range(1, size)]


def score_kernel(n, *refs):
    blocks, frames_ref, out_ref = refs[:n], refs[n], refs[n + 1]
    step = pl.program_id(0)
    model = jnp.concatenate([ref[...] for ref in blocks], axis=0)
    wide = model.astype(jnp.float32)
    part = lax.dot_general(
        model, frames_ref[...], (((1,), (1,)), ((), ())), preferred_element_type=jnp.float32
    ) - 0.5 * jnp.sum(wide * wide, axis=1, keepdims=True)

    @pl.when(step == 0)
    def _():
        out_ref[...] = part

    @pl.when(step > 0)
    def _():
        out_ref[...] += part


def score_parts(blocks, frames, tile):
    rows, pix = frames.shape
    many = sum(b.shape[0] for b in blocks)
    return pl.pallas_call(
        functools.partial(score_kernel, len(blocks)),
        grid=(pix // tile,),
        in_specs=[pl.BlockSpec((b.shape[0], tile), lambda i: (0, i)) for b in blocks]
        + [pl.BlockSpec((rows, tile), lambda i: (0, i))],
        out_specs=pl.BlockSpec((many, rows), lambda i: (0, 0)),
        out_shape=jax.ShapeDtypeStruct((many, rows), jnp.float32),
        compiler_params=pltpu.CompilerParams(vmem_limit_bytes=VMEM_BYTES),
        cost_estimate=pl.CostEstimate(flops=2 * rows * pix * many, bytes_accessed=2 * rows * pix, transcendentals=0),
    )(*blocks, frames)


def total_kernel(n, heights, tiles, *refs):
    parts, prior_ref, frames_ref = refs[:n], refs[n], refs[n + 1]
    outs, weights_ref = refs[n + 2 : -1], refs[-1]
    step = pl.program_id(0)

    @pl.when(step == 0)
    def _():
        raw = tree_sum([ref[...] for ref in parts])
        scores = (3.0 / math.sqrt(PIX)) * raw + prior_ref[...]
        up = jnp.exp(scores - jnp.max(scores, axis=0, keepdims=True))
        weights_ref[...] = (up / jnp.sum(up, axis=0, keepdims=True)).astype(jnp.bfloat16)

    weights = weights_ref[...]
    tile = frames_ref.shape[1]
    total = jnp.dot(weights, frames_ref[...], preferred_element_type=jnp.float32).astype(jnp.bfloat16)
    low = 0
    for ref, height in zip(outs, heights):
        ref[:, pl.ds(pl.multiple_of(step * tile, tile), tile)] = total[low : low + height]
        low += height

    @pl.when(step == tiles - 1)
    def _():
        counts = jnp.sum(weights.astype(jnp.float32), axis=1, keepdims=True)
        high = counts.astype(jnp.bfloat16)
        rest = (counts - high.astype(jnp.float32)).astype(jnp.bfloat16)
        lane = lax.broadcasted_iota(jnp.int32, (counts.shape[0], TAIL), 1)
        both = jnp.where(lane < TAIL // 2, high.astype(jnp.float32), rest.astype(jnp.float32)).astype(jnp.bfloat16)
        low = 0
        for ref, height in zip(outs, heights):
            ref[:, tiles * tile :] = both[low : low + height]
            low += height


def block_totals(parts, prior, frames, heights, tile):
    rows, pix = frames.shape
    many = prior.shape[0]
    return pl.pallas_call(
        functools.partial(total_kernel, len(parts), heights, pix // tile),
        grid=(pix // tile,),
        in_specs=[pl.BlockSpec(p.shape, lambda i: (0, 0)) for p in parts]
        + [pl.BlockSpec(prior.shape, lambda i: (0, 0)), pl.BlockSpec((rows, tile), lambda i: (0, i))],
        out_specs=[pl.BlockSpec((h, pix + TAIL), lambda i: (0, 0)) for h in heights],
        out_shape=[jax.ShapeDtypeStruct((h, pix + TAIL), jnp.bfloat16) for h in heights],
        scratch_shapes=[pltpu.VMEM((many, rows), jnp.bfloat16)],
        compiler_params=pltpu.CompilerParams(vmem_limit_bytes=VMEM_BYTES),
        cost_estimate=pl.CostEstimate(
            flops=2 * rows * pix * many, bytes_accessed=2 * rows * pix, transcendentals=rows * many
        ),
    )(*parts, prior, frames)


def update_kernel(terms, owned_ref, out_ref):
    pix = owned_ref.shape[1]

    def total(low, high):
        pieces = [ref[..., low:high].astype(jnp.float32) for ref in terms]
        return tree_sum([jnp.sum(p, axis=0) if p.ndim == 3 else p for p in pieces])

    tail = total(pix, pix + TAIL)
    counts = tail[:, :1] + tail[:, TAIL // 2 : TAIL // 2 + 1]
    out_ref[...] = ((total(0, pix) + owned_ref[...].astype(jnp.float32)) / (counts + 1.0)).astype(out_ref.dtype)


def update(terms, owned, dtype):
    def kernel(*refs):
        update_kernel(refs[: len(terms)], refs[-2], refs[-1])

    return pl.pallas_call(
        kernel,
        out_shape=jax.ShapeDtypeStruct(owned.shape, dtype),
        compiler_params=pltpu.CompilerParams(vmem_limit_bytes=VMEM_BYTES),
        cost_estimate=pl.CostEstimate(flops=8 * owned.size, bytes_accessed=12 * owned.size, transcendentals=0),
    )(*terms, owned)


def local(sizes, frames, slices, log_prior, orient):
    along, across = sizes
    owned = slices.shape[0]
    tile = min(2048, frames.shape[1])
    direct = along <= DIRECT
    if direct:
        first = lax.axis_index("frame") * owned
        orient = lax.dynamic_slice_in_dim(jnp.concatenate([orient, orient]), first, orient.shape[0], 0)
    matches = orient[:, None] == jnp.arange(log_prior.shape[0], dtype=jnp.int32)[None, :]
    prior = jnp.sum(jnp.where(matches, log_prior[None, :], 0.0), axis=1, keepdims=True)
    owned_b = slices.astype(jnp.bfloat16)
    for step in range(ITERS):
        if direct:
            blocks = [owned_b] + spread(owned_b, "frame", along, -1)
            heights = [owned] * along
        else:
            blocks = [lax.all_gather(owned_b, "frame", axis=0, tiled=True)]
            heights = [owned * along]
        parts = exchange_all(score_parts(blocks, frames, tile), ("panel", "sub"), across)
        totals = block_totals(parts, prior, frames, heights, tile)
        if direct:
            terms = [totals[0]] + spread(list(totals), "frame", along, 1)
        else:
            whole = totals[0].reshape(along, owned, totals[0].shape[1])
            terms = [lax.all_to_all(whole, "frame", split_axis=0, concat_axis=0, tiled=False)]
        owned_b = update(terms, owned_b, jnp.bfloat16 if step + 1 < ITERS else jnp.float32)
    return owned_b


def solution(mesh):
    in_specs = (
        P(("groups", "frame"), ("panel", "sub")),
        P(("groups", "frame"), ("panel", "sub")),
        P(),
        P("groups"),
    )
    out_specs = P(("groups", "frame"), ("panel", "sub"))
    sizes = (mesh.shape["frame"], mesh.shape["panel"] * mesh.shape["sub"])
    return jax.shard_map(
        functools.partial(local, sizes), mesh=mesh, in_specs=in_specs, out_specs=out_specs, check_vma=False
    )
```

```python
import functools
import math

import jax
import jax.numpy as jnp
from jax import lax
from jax.experimental import pallas as pl
from jax.experimental.pallas import tpu as pltpu
from jax.sharding import PartitionSpec as P

PIX = 65536
ITERS = 2
TAIL = 128
VMEM_BYTES = 40 * 1024 * 1024
IN_VMEM = pl.BlockSpec(memory_space=pltpu.VMEM)


def params():
    return pltpu.CompilerParams(vmem_limit_bytes=VMEM_BYTES)


def tree_sum(terms):
    while len(terms) > 1:
        terms = [a + b for a, b in zip(terms[::2], terms[1::2])] + terms[len(terms) & ~1 :]
    return terms[0]


def chunks(size, most):
    step = math.gcd(size, most)
    return [pl.ds(at, step) for at in range(0, size, step)]


def rotate_rows(value, by):
    return value if by == 0 else jnp.concatenate([value[by:], value[:by]], axis=0)


def from_others(block, axis, size):
    return [lax.ppermute(block, axis, [((i + k) % size, i) for i in range(size)]) for k in range(1, size)]


def to_others(blocks, axis, size):
    return [lax.ppermute(blocks[k], axis, [(i, (i + k) % size) for i in range(size)]) for k in range(1, size)]


def exchange_all(part, axes, size):
    if size & (size - 1):
        return [lax.psum(part, axes)]
    return [part] + [lax.ppermute(part, axes, [(i, i ^ k) for i in range(size)]) for k in range(1, size)]


def load_kernel(frames_ref, here_ref, turned_ref, sems):
    pieces = chunks(frames_ref.shape[1], 2048)
    copies = [
        pltpu.make_async_copy(frames_ref.at[:, piece], here_ref.at[:, piece], sems.at[i])
        for i, piece in enumerate(pieces)
    ]
    for copy in copies:
        copy.start()
    for copy, piece in zip(copies, pieces):
        copy.wait()
        turned_ref[piece, :] = here_ref[:, piece].T


def load_frames(frames):
    rows, pix = frames.shape
    return pl.pallas_call(
        load_kernel,
        in_specs=[pl.BlockSpec(memory_space=pl.ANY)],
        out_specs=[IN_VMEM, IN_VMEM],
        out_shape=[pltpu.VMEM((rows, pix), frames.dtype), pltpu.VMEM((pix, rows), frames.dtype)],
        scratch_shapes=[pltpu.SemaphoreType.DMA((len(chunks(pix, 2048)),))],
        compiler_params=params(),
        cost_estimate=pl.CostEstimate(flops=0, bytes_accessed=6 * rows * pix, transcendentals=0),
        name="load_frames",
    )(pltpu.with_memory_space_constraint(frames, pltpu.HBM))


def score_kernel(n, *refs):
    blocks, turned_ref, out_ref = refs[:n], refs[n], refs[n + 1]
    raw, squares = [], []
    for piece in chunks(turned_ref.shape[0], 512):
        model = jnp.concatenate([ref[:, piece] for ref in blocks], axis=0)
        raw.append(jnp.dot(model, turned_ref[piece, :], preferred_element_type=jnp.float32))
        wide = model.astype(jnp.float32)
        squares.append(tree_sum([jnp.square(wide[:, at : at + 128]) for at in range(0, wide.shape[1], 128)]))
        if len(raw) > 4:
            raw, squares = [raw[0] + raw[4], *raw[1:4]], [squares[0] + squares[4], *squares[1:4]]
            raw, squares = raw[1:] + raw[:1], squares[1:] + squares[:1]
    out_ref[...] = tree_sum(raw) - 0.5 * jnp.sum(tree_sum(squares), axis=1, keepdims=True)


def score_parts(blocks, turned):
    pix, rows = turned.shape
    many = sum(b.shape[0] for b in blocks)
    return pl.pallas_call(
        functools.partial(score_kernel, len(blocks)),
        in_specs=[IN_VMEM] * (len(blocks) + 1),
        out_specs=IN_VMEM,
        out_shape=jax.ShapeDtypeStruct((many, rows), jnp.float32),
        compiler_params=params(),
        cost_estimate=pl.CostEstimate(flops=2 * rows * pix * many, bytes_accessed=2 * rows * pix, transcendentals=0),
        name="score_parts",
    )(*blocks, pltpu.with_memory_space_constraint(turned, pltpu.VMEM))


def weigh(parts, prior_ref):
    raw = tree_sum([ref[...] for ref in parts])
    scores = (3.0 / math.sqrt(PIX)) * raw + prior_ref[...]
    up = jnp.exp(scores - jnp.max(scores, axis=0, keepdims=True))
    weights = (up / jnp.sum(up, axis=0, keepdims=True)).astype(jnp.bfloat16).astype(jnp.float32)
    counts = jnp.sum(weights, axis=1, keepdims=True)
    high = counts.astype(jnp.bfloat16).astype(jnp.float32)
    lane = lax.broadcasted_iota(jnp.int32, (counts.shape[0], TAIL), 1)
    return weights, jnp.where(lane < TAIL // 2, high, counts - high)


def plain_totals_kernel(n, *refs):
    parts, prior_ref, frames_ref, out_ref = refs[:n], refs[n], refs[n + 1], refs[n + 2]
    weights, tail = weigh(parts, prior_ref)
    weights = weights.astype(jnp.bfloat16)
    pix = frames_ref.shape[1]
    for piece in chunks(pix, 512):
        total = jnp.dot(weights, frames_ref[:, piece], preferred_element_type=jnp.float32)
        out_ref[:, piece] = total.astype(jnp.bfloat16)
    out_ref[:, pix:] = tail.astype(jnp.bfloat16)


def dense_totals_kernel(n, *refs):
    parts, prior_ref, frames_ref, outs = refs[:n], refs[n], refs[n + 1], refs[n + 2 :]
    weights, tail = weigh(parts, prior_ref)
    turned = [rotate_rows(weights, (-4 * q) % 16).astype(jnp.bfloat16) for q in range(4)]
    quarter = frames_ref.shape[1] // 4
    for piece in chunks(quarter, 512):
        totals = [
            jnp.dot(
                turned[q], frames_ref[:, pl.ds(q * quarter + piece.start, piece.size)], preferred_element_type=jnp.float32
            )
            for q in range(4)
        ]
        upper = lax.broadcasted_iota(jnp.int32, (8, piece.size), 0) < 4
        for k, out_ref in enumerate(outs):
            first = jnp.where(upper, totals[-k % 4][:8], totals[(1 - k) % 4][:8])
            second = jnp.where(upper, totals[(2 - k) % 4][8:], totals[(3 - k) % 4][8:])
            out_ref[:, piece] = jnp.concatenate([first, second], axis=0).astype(jnp.bfloat16)
    for k, out_ref in enumerate(outs):
        out_ref[:, quarter:] = jnp.concatenate([tail[4 * k : 4 * k + 4]] * 4, axis=0).astype(jnp.bfloat16)


def block_totals(parts, prior, frames, dense):
    rows, pix = frames.shape
    many = prior.shape[0]
    if dense:
        kernel, shapes = dense_totals_kernel, [(16, pix // 4 + TAIL)] * 4
    else:
        kernel, shapes = plain_totals_kernel, [(many, pix + TAIL)]
    return pl.pallas_call(
        functools.partial(kernel, len(parts)),
        in_specs=[IN_VMEM] * (len(parts) + 2),
        out_specs=[IN_VMEM] * len(shapes),
        out_shape=[jax.ShapeDtypeStruct(shape, jnp.bfloat16) for shape in shapes],
        compiler_params=params(),
        cost_estimate=pl.CostEstimate(
            flops=2 * rows * pix * many, bytes_accessed=2 * rows * pix, transcendentals=rows * many
        ),
        name="block_totals",
    )(*parts, prior, pltpu.with_memory_space_constraint(frames, pltpu.VMEM))


def plain_update_kernel(terms_ref, owned_ref, out_ref):
    pix = owned_ref.shape[1]
    tail = jnp.sum(terms_ref[:, :, pix:].astype(jnp.float32), axis=0)
    counts = tail[:, :1] + tail[:, TAIL // 2 : TAIL // 2 + 1]
    for piece in chunks(pix, 512):
        total = jnp.sum(terms_ref[:, :, piece].astype(jnp.float32), axis=0)
        out_ref[:, piece] = ((total + owned_ref[:, piece].astype(jnp.float32)) / (counts + 1.0)).astype(out_ref.dtype)


def dense_update_kernel(*refs):
    terms, owned_ref, out_ref = refs[:4], refs[4], refs[5]
    quarter = owned_ref.shape[1] // 4

    def total(piece):
        return tree_sum([rotate_rows(ref[:, piece].astype(jnp.float32), 4 * k) for k, ref in enumerate(terms)])

    tail = total(pl.ds(quarter, TAIL))
    scale = tail[:, :1] + tail[:, TAIL // 2 : TAIL // 2 + 1] + 1.0
    for piece in chunks(quarter, 512):
        spots = [pl.ds(q * quarter + piece.start, piece.size) for q in range(4)]
        owned = jnp.concatenate([owned_ref[:, spot].astype(jnp.float32) for spot in spots], axis=0)
        new = (total(piece) + owned) / scale
        for q, spot in enumerate(spots):
            out_ref[:, spot] = new[4 * q : 4 * q + 4].astype(out_ref.dtype)


def update(terms, owned, dtype):
    return pl.pallas_call(
        dense_update_kernel if len(terms) == 4 else plain_update_kernel,
        in_specs=[IN_VMEM] * (len(terms) + 1),
        out_specs=IN_VMEM,
        out_shape=jax.ShapeDtypeStruct(owned.shape, dtype),
        compiler_params=params(),
        cost_estimate=pl.CostEstimate(flops=8 * owned.size, bytes_accessed=12 * owned.size, transcendentals=0),
        name="update",
    )(*terms, owned)


def local(sizes, frames, slices, log_prior, orient):
    along, across = sizes
    owned, pix = slices.shape
    dense = along == 4 and owned == 4 and pix % 512 == 0
    if dense:
        first = lax.axis_index("frame") * owned
        orient = lax.dynamic_slice_in_dim(jnp.concatenate([orient, orient]), first, orient.shape[0], 0)
    matches = orient[:, None] == jnp.arange(log_prior.shape[0], dtype=jnp.int32)[None, :]
    prior = jnp.sum(jnp.where(matches, log_prior[None, :], 0.0), axis=1, keepdims=True)
    owned_b = slices.astype(jnp.bfloat16)
    here, turned = load_frames(frames)
    for step in range(ITERS):
        if dense:
            blocks = [owned_b] + from_others(owned_b, "frame", along)
        else:
            blocks = [lax.all_gather(owned_b, "frame", axis=0, tiled=True)]
        parts = exchange_all(score_parts(blocks, turned), ("panel", "sub"), across)
        totals = block_totals(parts, prior, here, dense)
        if dense:
            terms = [totals[0]] + to_others(totals, "frame", along)
        else:
            whole = totals[0].reshape(along, owned, totals[0].shape[1])
            terms = [lax.all_to_all(whole, "frame", split_axis=0, concat_axis=0, tiled=False)]
        owned_b = update(terms, owned_b, jnp.bfloat16 if step + 1 < ITERS else jnp.float32)
    return owned_b


def solution(mesh):
    in_specs = (
        P(("groups", "frame"), ("panel", "sub")),
        P(("groups", "frame"), ("panel", "sub")),
        P(),
        P("groups"),
    )
    out_specs = P(("groups", "frame"), ("panel", "sub"))
    sizes = (mesh.shape["frame"], mesh.shape["panel"] * mesh.shape["sub"])
    return jax.shard_map(
        functools.partial(local, sizes), mesh=mesh, in_specs=in_specs, out_specs=out_specs, check_vma=False
    )
```

```python
import functools
import math

import jax
import jax.numpy as jnp
from jax import lax
from jax.experimental import pallas as pl
from jax.experimental.pallas import tpu as pltpu
from jax.sharding import PartitionSpec as P

PIX = 65536
ITERS = 2
TAIL = 128
VMEM_BYTES = 12 * 1024 * 1024
IN_VMEM = pl.BlockSpec(memory_space=pltpu.VMEM)


def params():
    return pltpu.CompilerParams(vmem_limit_bytes=VMEM_BYTES)


def tree_sum(terms):
    while len(terms) > 1:
        terms = [a + b for a, b in zip(terms[::2], terms[1::2])] + terms[len(terms) & ~1 :]
    return terms[0]


def chunks(size, most):
    step = math.gcd(size, most)
    return [pl.ds(at, step) for at in range(0, size, step)]


def rotate_rows(value, by):
    return value if by == 0 else jnp.concatenate([value[by:], value[:by]], axis=0)


def from_others(block, axis, size):
    return [lax.ppermute(block, axis, [((i + k) % size, i) for i in range(size)]) for k in range(1, size)]


def to_others(blocks, axis, size):
    return [lax.ppermute(blocks[k], axis, [(i, (i + k) % size) for i in range(size)]) for k in range(1, size)]


def exchange_all(part, axes, size):
    if size & (size - 1):
        return [lax.psum(part, axes)]
    return [part] + [lax.ppermute(part, axes, [(i, i ^ k) for i in range(size)]) for k in range(1, size)]


def prior_kernel(turn, orient_ref, log_prior_ref, out_ref):
    many, columns = out_ref.shape
    first = lax.axis_index("frame") * turn
    for row in range(many):
        entry = log_prior_ref[orient_ref[lax.rem(first + row, many)]]
        out_ref[row : row + 1, :] = jnp.full((1, columns), entry, jnp.float32)


def slice_priors(orient, log_prior, turn, columns):
    return pl.pallas_call(
        functools.partial(prior_kernel, turn),
        in_specs=[pl.BlockSpec(memory_space=pltpu.SMEM)] * 2,
        out_specs=IN_VMEM,
        out_shape=jax.ShapeDtypeStruct((orient.shape[0], columns), jnp.float32),
        compiler_params=params(),
        cost_estimate=pl.CostEstimate(flops=0, bytes_accessed=4 * log_prior.size, transcendentals=0),
        name="slice_priors",
    )(orient, log_prior)


def load_kernel(frames_ref, here_ref, turned_ref, sems):
    pieces = chunks(frames_ref.shape[1], 2048)
    copies = [
        pltpu.make_async_copy(frames_ref.at[:, piece], here_ref.at[:, piece], sems.at[i])
        for i, piece in enumerate(pieces)
    ]
    for copy in copies:
        copy.start()
    for copy, piece in zip(copies, pieces):
        copy.wait()
        turned_ref[piece, :] = here_ref[:, piece].T


def load_frames(frames):
    rows, pix = frames.shape
    return pl.pallas_call(
        load_kernel,
        in_specs=[pl.BlockSpec(memory_space=pl.ANY)],
        out_specs=[IN_VMEM, IN_VMEM],
        out_shape=[pltpu.VMEM((rows, pix), frames.dtype), pltpu.VMEM((pix, rows), frames.dtype)],
        scratch_shapes=[pltpu.SemaphoreType.DMA((len(chunks(pix, 2048)),))],
        compiler_params=params(),
        cost_estimate=pl.CostEstimate(flops=0, bytes_accessed=6 * rows * pix, transcendentals=0),
        name="load_frames",
    )(pltpu.with_memory_space_constraint(frames, pltpu.HBM))


def score_kernel(n, *refs):
    blocks, turned_ref, out_ref = refs[:n], refs[n], refs[n + 1]
    raw, squares = [], []
    for piece in chunks(turned_ref.shape[0], 512):
        model = jnp.concatenate([ref[:, piece] for ref in blocks], axis=0)
        raw.append(jnp.dot(model, turned_ref[piece, :], preferred_element_type=jnp.float32))
        wide = model.astype(jnp.float32)
        squares.append(tree_sum([jnp.square(wide[:, at : at + 128]) for at in range(0, wide.shape[1], 128)]))
        if len(raw) > 4:
            raw, squares = [raw[0] + raw[4], *raw[1:4]], [squares[0] + squares[4], *squares[1:4]]
            raw, squares = raw[1:] + raw[:1], squares[1:] + squares[:1]
    out_ref[...] = tree_sum(raw) - 0.5 * jnp.sum(tree_sum(squares), axis=1, keepdims=True)


def score_parts(blocks, turned):
    pix, rows = turned.shape
    many = sum(b.shape[0] for b in blocks)
    return pl.pallas_call(
        functools.partial(score_kernel, len(blocks)),
        in_specs=[IN_VMEM] * (len(blocks) + 1),
        out_specs=IN_VMEM,
        out_shape=jax.ShapeDtypeStruct((many, rows), jnp.float32),
        compiler_params=params(),
        cost_estimate=pl.CostEstimate(flops=2 * rows * pix * many, bytes_accessed=2 * rows * pix, transcendentals=0),
        name="score_parts",
    )(*blocks, pltpu.with_memory_space_constraint(turned, pltpu.VMEM))


def weigh(parts, prior_ref):
    raw = tree_sum([ref[...] for ref in parts])
    scores = (3.0 / math.sqrt(PIX)) * raw + prior_ref[...]
    up = jnp.exp(scores - jnp.max(scores, axis=0, keepdims=True))
    weights = (up / jnp.sum(up, axis=0, keepdims=True)).astype(jnp.bfloat16).astype(jnp.float32)
    counts = jnp.sum(weights, axis=1, keepdims=True)
    high = counts.astype(jnp.bfloat16).astype(jnp.float32)
    lane = lax.broadcasted_iota(jnp.int32, (counts.shape[0], TAIL), 1)
    return weights, jnp.where(lane < TAIL // 2, high, counts - high)


def plain_totals_kernel(n, *refs):
    parts, prior_ref, frames_ref, out_ref = refs[:n], refs[n], refs[n + 1], refs[n + 2]
    weights, tail = weigh(parts, prior_ref)
    weights = weights.astype(jnp.bfloat16)
    pix = frames_ref.shape[1]
    for piece in chunks(pix, 512):
        total = jnp.dot(weights, frames_ref[:, piece], preferred_element_type=jnp.float32)
        out_ref[:, piece] = total.astype(jnp.bfloat16)
    out_ref[:, pix:] = tail.astype(jnp.bfloat16)


def dense_totals_kernel(n, *refs):
    parts, prior_ref, frames_ref, outs = refs[:n], refs[n], refs[n + 1], refs[n + 2 :]
    weights, tail = weigh(parts, prior_ref)
    turned = [rotate_rows(weights, (-4 * q) % 16).astype(jnp.bfloat16) for q in range(4)]
    quarter = frames_ref.shape[1] // 4
    for piece in chunks(quarter, 512):
        totals = [
            jnp.dot(
                turned[q], frames_ref[:, pl.ds(q * quarter + piece.start, piece.size)], preferred_element_type=jnp.float32
            )
            for q in range(4)
        ]
        upper = lax.broadcasted_iota(jnp.int32, (8, piece.size), 0) < 4
        for k, out_ref in enumerate(outs):
            first = jnp.where(upper, totals[-k % 4][:8], totals[(1 - k) % 4][:8])
            second = jnp.where(upper, totals[(2 - k) % 4][8:], totals[(3 - k) % 4][8:])
            out_ref[:, piece] = jnp.concatenate([first, second], axis=0).astype(jnp.bfloat16)
    for k, out_ref in enumerate(outs):
        out_ref[:, quarter:] = jnp.concatenate([tail[4 * k : 4 * k + 4]] * 4, axis=0).astype(jnp.bfloat16)


def block_totals(parts, prior, frames, dense):
    rows, pix = frames.shape
    many = prior.shape[0]
    if dense:
        kernel, shapes = dense_totals_kernel, [(16, pix // 4 + TAIL)] * 4
    else:
        kernel, shapes = plain_totals_kernel, [(many, pix + TAIL)]
    return pl.pallas_call(
        functools.partial(kernel, len(parts)),
        in_specs=[IN_VMEM] * (len(parts) + 2),
        out_specs=[IN_VMEM] * len(shapes),
        out_shape=[jax.ShapeDtypeStruct(shape, jnp.bfloat16) for shape in shapes],
        compiler_params=params(),
        cost_estimate=pl.CostEstimate(
            flops=2 * rows * pix * many, bytes_accessed=2 * rows * pix, transcendentals=rows * many
        ),
        name="block_totals",
    )(*parts, prior, pltpu.with_memory_space_constraint(frames, pltpu.VMEM))


def plain_update_kernel(terms_ref, owned_ref, out_ref):
    pix = owned_ref.shape[1]
    tail = jnp.sum(terms_ref[:, :, pix:].astype(jnp.float32), axis=0)
    counts = tail[:, :1] + tail[:, TAIL // 2 : TAIL // 2 + 1]
    for piece in chunks(pix, 512):
        total = jnp.sum(terms_ref[:, :, piece].astype(jnp.float32), axis=0)
        out_ref[:, piece] = ((total + owned_ref[:, piece].astype(jnp.float32)) / (counts + 1.0)).astype(out_ref.dtype)


def dense_update_kernel(*refs):
    terms, owned_ref, out_ref = refs[:4], refs[4], refs[5]
    quarter = owned_ref.shape[1] // 4

    def total(piece):
        return tree_sum([rotate_rows(ref[:, piece].astype(jnp.float32), 4 * k) for k, ref in enumerate(terms)])

    tail = total(pl.ds(quarter, TAIL))
    scale = tail[:, :1] + tail[:, TAIL // 2 : TAIL // 2 + 1] + 1.0
    for piece in chunks(quarter, 512):
        spots = [pl.ds(q * quarter + piece.start, piece.size) for q in range(4)]
        owned = jnp.concatenate([owned_ref[:, spot].astype(jnp.float32) for spot in spots], axis=0)
        new = (total(piece) + owned) / scale
        for q, spot in enumerate(spots):
            out_ref[:, spot] = new[4 * q : 4 * q + 4].astype(out_ref.dtype)


def update(terms, owned, dtype):
    return pl.pallas_call(
        dense_update_kernel if len(terms) == 4 else plain_update_kernel,
        in_specs=[IN_VMEM] * (len(terms) + 1),
        out_specs=IN_VMEM,
        out_shape=jax.ShapeDtypeStruct(owned.shape, dtype),
        compiler_params=params(),
        cost_estimate=pl.CostEstimate(flops=8 * owned.size, bytes_accessed=12 * owned.size, transcendentals=0),
        name="update",
    )(*terms, owned)


def local(sizes, frames, slices, log_prior, orient):
    along, across = sizes
    owned, pix = slices.shape
    dense = along == 4 and owned == 4 and pix % 512 == 0
    prior = slice_priors(orient, log_prior, owned if dense else 0, frames.shape[0])
    owned_b = slices.astype(jnp.bfloat16)
    frames, prior = lax.optimization_barrier((frames, prior))
    here, turned = load_frames(frames)
    for step in range(ITERS):
        if dense:
            blocks = [owned_b] + from_others(owned_b, "frame", along)
        else:
            blocks = [lax.all_gather(owned_b, "frame", axis=0, tiled=True)]
        parts = exchange_all(score_parts(blocks, turned), ("panel", "sub"), across)
        totals = block_totals(parts, prior, here, dense)
        if dense:
            terms = [totals[0]] + to_others(totals, "frame", along)
        else:
            whole = totals[0].reshape(along, owned, totals[0].shape[1])
            terms = [lax.all_to_all(whole, "frame", split_axis=0, concat_axis=0, tiled=False)]
        owned_b = update(terms, owned_b, jnp.bfloat16 if step + 1 < ITERS else jnp.float32)
    return owned_b


def solution(mesh):
    in_specs = (
        P(("groups", "frame"), ("panel", "sub")),
        P(("groups", "frame"), ("panel", "sub")),
        P(),
        P("groups"),
    )
    out_specs = P(("groups", "frame"), ("panel", "sub"))
    sizes = (mesh.shape["frame"], mesh.shape["panel"] * mesh.shape["sub"])
    return jax.shard_map(
        functools.partial(local, sizes), mesh=mesh, in_specs=in_specs, out_specs=out_specs, check_vma=False
    )
```

```python
import functools
import math

import jax
import jax.numpy as jnp
from jax import lax
from jax.experimental import pallas as pl
from jax.experimental.pallas import tpu as pltpu
from jax.sharding import PartitionSpec as P

PIX = 65536
ITERS = 2
GATHER_ORDER = (0, 1, 2, 3, 4, 5)
SCATTER_ORDER = (0, 1, 2, 3, 4)
TAIL = 128
VMEM_BYTES = 12 * 1024 * 1024
IN_VMEM = pl.BlockSpec(memory_space=pltpu.VMEM)


def params():
    return pltpu.CompilerParams(vmem_limit_bytes=VMEM_BYTES)


def tree_sum(terms):
    while len(terms) > 1:
        terms = [a + b for a, b in zip(terms[::2], terms[1::2])] + terms[len(terms) & ~1 :]
    return terms[0]


def chunks(size, most):
    step = math.gcd(size, most)
    return [pl.ds(at, step) for at in range(0, size, step)]


def rotate_rows(value, by):
    return value if by == 0 else jnp.concatenate([value[by:], value[:by]], axis=0)


def early(value, flops):
    return pl.pallas_call(
        lambda in_ref, out_ref: None,
        in_specs=[pl.BlockSpec(memory_space=pl.ANY)],
        out_specs=pl.BlockSpec(memory_space=pl.ANY),
        out_shape=jax.ShapeDtypeStruct(value.shape, value.dtype),
        input_output_aliases={0: 0},
        compiler_params=params(),
        cost_estimate=pl.CostEstimate(flops=flops, bytes_accessed=0, transcendentals=0),
        name="early",
    )(value)


def swap(value, distance):
    return lax.ppermute(value, "frame", [(i, i ^ distance) for i in range(4)])


def gather_line(whole, relayed, direct):
    over = swap(relayed, 2)
    direct_2 = swap(direct, 2)
    direct_3 = swap(direct, 3)
    near = swap(whole, 1)
    return [whole, near, over, direct_2, swap(over, 1), direct_3], over


def round_kernel(slices_ref, whole_ref, first_ref, second_ref, held_ref, sems):
    pix = slices_ref.shape[1]
    quarter, half = pix // 4, pix // 8
    copies = [
        pltpu.make_async_copy(
            slices_ref.at[:, pl.ds(q * quarter, quarter)], held_ref.at[:, pl.ds(q * quarter, quarter)], sems.at[q]
        )
        for q in range(4)
    ]
    for copy in copies:
        copy.start()
    for q, copy in enumerate(copies):
        copy.wait()
        for part, out_ref in enumerate((first_ref, second_ref)):
            there = pl.ds(q * quarter + part * half, half)
            value = held_ref[:, there].astype(jnp.bfloat16)
            whole_ref[:, there] = value
            out_ref[:, pl.ds(q * half, half)] = value


def round_slices(slices):
    owned, pix = slices.shape
    return pl.pallas_call(
        round_kernel,
        in_specs=[pl.BlockSpec(memory_space=pl.ANY)],
        out_specs=[IN_VMEM] * 3,
        out_shape=[jax.ShapeDtypeStruct((owned, size), jnp.bfloat16) for size in (pix, pix // 2, pix // 2)],
        scratch_shapes=[pltpu.VMEM((owned, pix), slices.dtype), pltpu.SemaphoreType.DMA((4,))],
        compiler_params=params(),
        cost_estimate=pl.CostEstimate(flops=0, bytes_accessed=8 * slices.size, transcendentals=0),
        name="round_slices",
    )(pltpu.with_memory_space_constraint(slices, pltpu.HBM))


def relay_kernel(came_ref, own_ref, out_ref):
    for piece in chunks(own_ref.shape[1], 512):
        came = rotate_rows(came_ref[:, piece].astype(jnp.float32), 4)
        out_ref[:, piece] = (came + own_ref[:, piece].astype(jnp.float32)).astype(jnp.bfloat16)


def scatter_line(own, near, relayed_2, direct_2, relayed_3, direct_3):
    came = swap(relayed_3, 1)
    joined = pl.pallas_call(
        relay_kernel,
        in_specs=[IN_VMEM] * 2,
        out_specs=IN_VMEM,
        out_shape=jax.ShapeDtypeStruct(came.shape, came.dtype),
        compiler_params=params(),
        cost_estimate=pl.CostEstimate(flops=2 * came.size, bytes_accessed=6 * came.size, transcendentals=0),
        name="relay",
    )(came, relayed_2)
    joined = swap(joined, 2)
    direct_3 = early(swap(direct_3, 3), 10**9)
    direct_2 = early(swap(direct_2, 2), 10**9)
    near = swap(near, 1)
    return [own, near, joined, direct_2, direct_3]


def exchange_all(part, axes, size):
    if size & (size - 1):
        return [lax.psum(part, axes)]
    return [part] + [lax.ppermute(part, axes, [(i, i ^ k) for i in range(size)]) for k in range(1, size)]


def load_kernel(
    dense, frames_ref, orient_in_ref, log_prior_in_ref, here_ref, turned_ref, prior_ref, orient_ref, log_prior_ref, sems
):
    pieces = chunks(frames_ref.shape[1], 2048)
    tables = [
        pltpu.make_async_copy(orient_in_ref, orient_ref, sems.at[len(pieces)]),
        pltpu.make_async_copy(log_prior_in_ref, log_prior_ref, sems.at[len(pieces) + 1]),
    ]
    for copy in tables:
        copy.start()
    copies = [
        pltpu.make_async_copy(frames_ref.at[:, piece], here_ref.at[:, piece], sems.at[i])
        for i, piece in enumerate(pieces)
    ]
    for copy in copies:
        copy.start()
    for i, (copy, piece) in enumerate(zip(copies, pieces)):
        copy.wait()
        turned_ref[piece, :] = here_ref[:, piece].T
        if i == len(pieces) // 2:
            for table in tables:
                table.wait()
            many, columns = prior_ref.shape
            place = lax.axis_index("frame")
            for row in range(many):
                spot = 4 * (place ^ (row // 4)) + row % 4 if dense else row
                prior_ref[row : row + 1, :] = jnp.full((1, columns), log_prior_ref[orient_ref[spot]], jnp.float32)


def load_frames(frames, orient, log_prior, dense):
    rows, pix = frames.shape
    return pl.pallas_call(
        functools.partial(load_kernel, dense),
        in_specs=[pl.BlockSpec(memory_space=pl.ANY)] * 3,
        out_specs=[IN_VMEM] * 3,
        out_shape=[
            pltpu.VMEM((rows, pix), frames.dtype),
            pltpu.VMEM((pix, rows), frames.dtype),
            jax.ShapeDtypeStruct((orient.shape[0], rows), jnp.float32),
        ],
        scratch_shapes=[
            pltpu.SMEM(orient.shape, orient.dtype),
            pltpu.SMEM(log_prior.shape, log_prior.dtype),
            pltpu.SemaphoreType.DMA((len(chunks(pix, 2048)) + 2,)),
        ],
        compiler_params=params(),
        cost_estimate=pl.CostEstimate(flops=0, bytes_accessed=6 * rows * pix, transcendentals=0),
        name="load_frames",
    )(*(pltpu.with_memory_space_constraint(x, pltpu.HBM) for x in (frames, orient, log_prior)))


def score_kernel(pieces, order, *refs):
    turned_ref, out_ref = refs[-2:]
    raw, squares = [], []
    for first, size, rows in pieces:
        model = jnp.concatenate([refs[order.index(ref)][:, pl.ds(column, size)] for ref, column in rows], axis=0)
        raw.append(jnp.dot(model, turned_ref[pl.ds(first, size), :], preferred_element_type=jnp.float32))
        wide = model.astype(jnp.float32)
        squares.append(tree_sum([jnp.square(wide[:, at : at + 128]) for at in range(0, wide.shape[1], 128)]))
        if len(raw) > 4:
            raw, squares = raw[1:4] + [raw[0] + raw[4]], squares[1:4] + [squares[0] + squares[4]]
    out_ref[...] = tree_sum(raw) - 0.5 * jnp.sum(tree_sum(squares), axis=1, keepdims=True)


def score_parts(blocks, pieces, many, turned):
    pix, rows = turned.shape
    order = GATHER_ORDER if len(blocks) > 1 else (0,)
    return pl.pallas_call(
        functools.partial(score_kernel, pieces, order),
        in_specs=[IN_VMEM] * (len(blocks) + 1),
        out_specs=IN_VMEM,
        out_shape=jax.ShapeDtypeStruct((many, rows), jnp.float32),
        compiler_params=params(),
        cost_estimate=pl.CostEstimate(flops=2 * rows * pix * many, bytes_accessed=2 * rows * pix, transcendentals=0),
        name="score_parts",
    )(*[blocks[i] for i in order], pltpu.with_memory_space_constraint(turned, pltpu.VMEM))


def gathered_pieces(pix):
    quarter = pix // 4
    half = quarter // 2
    pieces = []
    for part in range(2):
        for q in range(4):
            for at in range(0, half, math.gcd(half, 512)):
                there, here = q * quarter + part * half + at, q * half + at
                rows = [(0, there), (1, there), (2 + part, here), (4 + part, here)]
                pieces.append((there, math.gcd(half, 512), rows))
    return pieces


def weigh(parts, prior_ref):
    raw = tree_sum([ref[...] for ref in parts])
    scores = (3.0 / math.sqrt(PIX)) * raw + prior_ref[...]
    up = jnp.exp(scores - jnp.max(scores, axis=0, keepdims=True))
    weights = (up / jnp.sum(up, axis=0, keepdims=True)).astype(jnp.bfloat16).astype(jnp.float32)
    counts = jnp.sum(weights, axis=1, keepdims=True)
    high = counts.astype(jnp.bfloat16).astype(jnp.float32)
    lane = lax.broadcasted_iota(jnp.int32, (counts.shape[0], TAIL), 1)
    return weights, jnp.where(lane < TAIL // 2, high, counts - high)


def plain_totals_kernel(n, *refs):
    parts, prior_ref, frames_ref, out_ref = refs[:n], refs[n], refs[n + 1], refs[n + 2]
    weights, tail = weigh(parts, prior_ref)
    weights = weights.astype(jnp.bfloat16)
    pix = frames_ref.shape[1]
    for piece in chunks(pix, 512):
        total = jnp.dot(weights, frames_ref[:, piece], preferred_element_type=jnp.float32)
        out_ref[:, piece] = total.astype(jnp.bfloat16)
    out_ref[:, pix:] = tail.astype(jnp.bfloat16)


def dense_totals_kernel(n, *refs):
    parts, prior_ref, frames_ref, outs = refs[:n], refs[n], refs[n + 1], refs[n + 2 :]
    weights, tail = weigh(parts, prior_ref)
    quarter = frames_ref.shape[1] // 4
    half = quarter // 2
    for k, out_ref in enumerate([outs[0], outs[1], outs[3], outs[5]]):
        rows = jnp.concatenate([tail[4 * k : 4 * k + 4]] * 4, axis=0)
        out_ref[:, out_ref.shape[1] - TAIL :] = rows.astype(jnp.bfloat16)
    turned = [rotate_rows(weights, (-4 * q) % 16).astype(jnp.bfloat16) for q in range(4)]
    for part in range(2):
        for piece in chunks(half, 512):
            totals = [
                jnp.dot(
                    turned[q],
                    frames_ref[:, pl.ds(q * quarter + part * half + piece.start, piece.size)],
                    preferred_element_type=jnp.float32,
                )
                for q in range(4)
            ]
            upper = lax.broadcasted_iota(jnp.int32, (8, piece.size), 0) < 4
            whole = pl.ds(part * half + piece.start, piece.size)
            spots = [(outs[0], whole), (outs[1], whole), (outs[2 + part], piece), (outs[4 + part], piece)]
            for k, (out_ref, spot) in enumerate(spots):
                first = jnp.where(upper, totals[-k % 4][:8], totals[(1 - k) % 4][:8])
                second = jnp.where(upper, totals[(2 - k) % 4][8:], totals[(3 - k) % 4][8:])
                out_ref[:, spot] = jnp.concatenate([first, second], axis=0).astype(jnp.bfloat16)


def block_totals(parts, prior, frames, dense):
    rows, pix = frames.shape
    many = prior.shape[0]
    if dense:
        half = pix // 8
        kernel = dense_totals_kernel
        shapes = [(16, 2 * half + TAIL)] * 2 + [(16, half), (16, half + TAIL)] * 2
    else:
        kernel, shapes = plain_totals_kernel, [(many, pix + TAIL)]
    return pl.pallas_call(
        functools.partial(kernel, len(parts)),
        in_specs=[IN_VMEM] * (len(parts) + 2),
        out_specs=[IN_VMEM] * len(shapes),
        out_shape=[jax.ShapeDtypeStruct(shape, jnp.bfloat16) for shape in shapes],
        compiler_params=params(),
        cost_estimate=pl.CostEstimate(
            flops=2 * rows * pix * many, bytes_accessed=2 * rows * pix, transcendentals=rows * many
        ),
        name="block_totals",
    )(*parts, prior, pltpu.with_memory_space_constraint(frames, pltpu.VMEM))


def plain_update_kernel(terms_ref, owned_ref, out_ref):
    pix = owned_ref.shape[1]
    tail = jnp.sum(terms_ref[:, :, pix:].astype(jnp.float32), axis=0)
    counts = tail[:, :1] + tail[:, TAIL // 2 : TAIL // 2 + 1]
    for piece in chunks(pix, 512):
        total = jnp.sum(terms_ref[:, :, piece].astype(jnp.float32), axis=0)
        out_ref[:, piece] = ((total + owned_ref[:, piece].astype(jnp.float32)) / (counts + 1.0)).astype(out_ref.dtype)


def dense_update_kernel(*refs):
    own_ref, near_ref, joined_ref, direct_2_ref, direct_3_ref = (refs[SCATTER_ORDER.index(i)] for i in range(5))
    owned_ref, out_ref = refs[5:7]
    quarter = owned_ref.shape[1] // 4
    half = quarter // 2

    def total(terms):
        return tree_sum([rotate_rows(ref[:, spot].astype(jnp.float32), 4 * k) for k, ref, spot in terms])

    behind, behind_half = pl.ds(quarter, TAIL), pl.ds(half, TAIL)
    tail = total(
        [(0, own_ref, behind), (1, near_ref, behind), (2, direct_2_ref, behind_half), (3, direct_3_ref, behind_half)]
    )
    scale = tail[:, :1] + tail[:, TAIL // 2 : TAIL // 2 + 1] + 1.0
    for part in range(2):
        for piece in chunks(half, 512):
            whole = pl.ds(part * half + piece.start, piece.size)
            terms = [(0, own_ref, whole), (1, near_ref, whole)]
            terms += [(2, direct_2_ref, piece), (3, direct_3_ref, piece)] if part else [(2, joined_ref, piece)]
            spots = [pl.ds(q * quarter + whole.start, whole.size) for q in range(4)]
            owned = jnp.concatenate([owned_ref[:, spot].astype(jnp.float32) for spot in spots], axis=0)
            new = ((total(terms) + owned) / scale).astype(out_ref.dtype)
            for q, spot in enumerate(spots):
                out_ref[:, spot] = new[4 * q : 4 * q + 4]
                if len(refs) > 7:
                    refs[7 + part][:, pl.ds(q * half + piece.start, piece.size)] = new[4 * q : 4 * q + 4]


def update(terms, owned, dtype, halves):
    shapes = [owned.shape] + ([(owned.shape[0], owned.shape[1] // 2)] * 2 if halves else [])
    return pl.pallas_call(
        plain_update_kernel if len(terms) == 1 else dense_update_kernel,
        in_specs=[IN_VMEM] * (len(terms) + 1),
        out_specs=[IN_VMEM] * len(shapes),
        out_shape=[jax.ShapeDtypeStruct(shape, dtype) for shape in shapes],
        compiler_params=params(),
        cost_estimate=pl.CostEstimate(flops=8 * owned.size, bytes_accessed=12 * owned.size, transcendentals=0),
        name="update",
    )(*([terms[i] for i in SCATTER_ORDER] if len(terms) > 1 else terms), owned)


def local(sizes, frames, slices, log_prior, orient):
    along, across = sizes
    owned, pix = slices.shape
    dense = along == 4 and owned == 4 and pix % 2048 == 0
    owned_b = round_slices(slices) if dense else [slices.astype(jnp.bfloat16)]
    if not dense:
        here, turned, prior = load_frames(frames, orient, log_prior, dense)
    for step in range(ITERS):
        last = step + 1 == ITERS
        if dense:
            blocks, over = gather_line(*owned_b)
            if step == 0:
                frames, over = lax.optimization_barrier((frames, over))
                here, turned, prior = load_frames(frames, orient, log_prior, dense)
            pieces = gathered_pieces(pix)
        else:
            blocks = [lax.all_gather(owned_b[0], "frame", axis=0, tiled=True)]
            pieces = [(piece.start, piece.size, [(0, piece.start)]) for piece in chunks(pix, 512)]
        parts = exchange_all(
            score_parts(blocks, pieces, along * owned, turned), ("panel", "sub"), across
        )
        totals = block_totals(parts, prior, here, dense)
        if dense:
            terms = scatter_line(*totals)
        else:
            whole = totals[0].reshape(along, owned, totals[0].shape[1])
            terms = [lax.all_to_all(whole, "frame", split_axis=0, concat_axis=0, tiled=False)]
        owned_b = update(terms, owned_b[0], jnp.float32 if last else jnp.bfloat16, dense and not last)
    return owned_b[0]


def solution(mesh):
    in_specs = (
        P(("groups", "frame"), ("panel", "sub")),
        P(("groups", "frame"), ("panel", "sub")),
        P(),
        P("groups"),
    )
    out_specs = P(("groups", "frame"), ("panel", "sub"))
    sizes = (mesh.shape["frame"], mesh.shape["panel"] * mesh.shape["sub"])
    return jax.shard_map(
        functools.partial(local, sizes), mesh=mesh, in_specs=in_specs, out_specs=out_specs, check_vma=False
    )
```

```python
import functools
import math

import jax
import jax.numpy as jnp
from jax import lax
from jax.experimental import pallas as pl
from jax.experimental.pallas import tpu as pltpu
from jax.sharding import PartitionSpec as P

PIX = 65536
ITERS = 2
GATHER_ORDER = (0, 1, 2, 3, 4, 5)
SCATTER_ORDER = (0, 1, 2, 3, 4)
TAIL = 128
VMEM_BYTES = 12 * 1024 * 1024
IN_VMEM = pl.BlockSpec(memory_space=pltpu.VMEM)


def params():
    return pltpu.CompilerParams(vmem_limit_bytes=VMEM_BYTES)


def tree_sum(terms):
    while len(terms) > 1:
        terms = [a + b for a, b in zip(terms[::2], terms[1::2])] + terms[len(terms) & ~1 :]
    return terms[0]


def chunks(size, most):
    step = math.gcd(size, most)
    return [pl.ds(at, step) for at in range(0, size, step)]


def rotate_rows(value, by):
    return value if by == 0 else jnp.concatenate([value[by:], value[:by]], axis=0)


def early(value, flops):
    return pl.pallas_call(
        lambda in_ref, out_ref: None,
        in_specs=[pl.BlockSpec(memory_space=pl.ANY)],
        out_specs=pl.BlockSpec(memory_space=pl.ANY),
        out_shape=jax.ShapeDtypeStruct(value.shape, value.dtype),
        input_output_aliases={0: 0},
        compiler_params=params(),
        cost_estimate=pl.CostEstimate(flops=flops, bytes_accessed=0, transcendentals=0),
        name="early",
    )(value)


def swap(value, distance):
    return lax.ppermute(value, "frame", [(i, i ^ distance) for i in range(4)])


def gather_line(whole, relayed, direct):
    over = swap(relayed, 2)
    direct_2 = swap(direct, 2)
    direct_3 = swap(direct, 3)
    near = swap(whole, 1)
    return [whole, near, over, direct_2, swap(over, 1), direct_3], over


def round_kernel(slices_ref, whole_ref, first_ref, second_ref, held_ref, sems):
    pix = slices_ref.shape[1]
    quarter, half = pix // 4, pix // 8
    copies = [
        pltpu.make_async_copy(
            slices_ref.at[:, pl.ds(q * quarter, quarter)], held_ref.at[:, pl.ds(q * quarter, quarter)], sems.at[q]
        )
        for q in range(4)
    ]
    for copy in copies:
        copy.start()
    for q, copy in enumerate(copies):
        copy.wait()
        for part, out_ref in enumerate((first_ref, second_ref)):
            there = pl.ds(q * quarter + part * half, half)
            value = held_ref[:, there].astype(jnp.bfloat16)
            whole_ref[:, there] = value
            out_ref[:, pl.ds(q * half, half)] = value


def round_slices(slices):
    owned, pix = slices.shape
    return pl.pallas_call(
        round_kernel,
        in_specs=[pl.BlockSpec(memory_space=pl.ANY)],
        out_specs=[IN_VMEM] * 3,
        out_shape=[jax.ShapeDtypeStruct((owned, size), jnp.bfloat16) for size in (pix, pix // 2, pix // 2)],
        scratch_shapes=[pltpu.VMEM((owned, pix), slices.dtype), pltpu.SemaphoreType.DMA((4,))],
        compiler_params=params(),
        cost_estimate=pl.CostEstimate(flops=0, bytes_accessed=8 * slices.size, transcendentals=0),
        name="round_slices",
    )(pltpu.with_memory_space_constraint(slices, pltpu.HBM))


def relay_kernel(came_ref, own_ref, out_ref):
    for piece in chunks(own_ref.shape[1], 512):
        came = rotate_rows(came_ref[:, piece].astype(jnp.float32), 4)
        out_ref[:, piece] = (came + own_ref[:, piece].astype(jnp.float32)).astype(jnp.bfloat16)


def scatter_line(own, near, relayed_2, direct_2, relayed_3, direct_3):
    came = swap(relayed_3, 1)
    joined = pl.pallas_call(
        relay_kernel,
        in_specs=[IN_VMEM] * 2,
        out_specs=IN_VMEM,
        out_shape=jax.ShapeDtypeStruct(came.shape, came.dtype),
        compiler_params=params(),
        cost_estimate=pl.CostEstimate(flops=2 * came.size, bytes_accessed=6 * came.size, transcendentals=0),
        name="relay",
    )(came, relayed_2)
    joined = swap(joined, 2)
    direct_3 = early(swap(direct_3, 3), 10**9)
    direct_2 = early(swap(direct_2, 2), 10**9)
    near = swap(near, 1)
    return [own, near, joined, direct_2, direct_3]


def exchange_all(part, axes, size):
    if size & (size - 1):
        return [lax.psum(part, axes)]
    return [part] + [lax.ppermute(part, axes, [(i, i ^ k) for i in range(size)]) for k in range(1, size)]


def load_kernel(
    dense, frames_ref, orient_in_ref, log_prior_in_ref, here_ref, turned_ref, prior_ref, orient_ref, log_prior_ref, sems
):
    pieces = chunks(frames_ref.shape[1], 2048)
    tables = [
        pltpu.make_async_copy(orient_in_ref, orient_ref, sems.at[len(pieces)]),
        pltpu.make_async_copy(log_prior_in_ref, log_prior_ref, sems.at[len(pieces) + 1]),
    ]
    for copy in tables:
        copy.start()
    copies = [
        pltpu.make_async_copy(frames_ref.at[:, piece], here_ref.at[:, piece], sems.at[i])
        for i, piece in enumerate(pieces)
    ]
    for copy in copies:
        copy.start()
    for i, (copy, piece) in enumerate(zip(copies, pieces)):
        copy.wait()
        turned_ref[piece, :] = here_ref[:, piece].T
        if i == len(pieces) // 2:
            for table in tables:
                table.wait()
            many, columns = prior_ref.shape
            place = lax.axis_index("frame")
            for row in range(many):
                spot = 4 * (place ^ (row // 4)) + row % 4 if dense else row
                prior_ref[row : row + 1, :] = jnp.full((1, columns), log_prior_ref[orient_ref[spot]], jnp.float32)


def load_frames(frames, orient, log_prior, dense):
    rows, pix = frames.shape
    return pl.pallas_call(
        functools.partial(load_kernel, dense),
        in_specs=[pl.BlockSpec(memory_space=pl.ANY)] * 3,
        out_specs=[IN_VMEM] * 3,
        out_shape=[
            pltpu.VMEM((rows, pix), frames.dtype),
            pltpu.VMEM((pix, rows), frames.dtype),
            jax.ShapeDtypeStruct((orient.shape[0], rows), jnp.float32),
        ],
        scratch_shapes=[
            pltpu.SMEM(orient.shape, orient.dtype),
            pltpu.SMEM(log_prior.shape, log_prior.dtype),
            pltpu.SemaphoreType.DMA((len(chunks(pix, 2048)) + 2,)),
        ],
        compiler_params=params(),
        cost_estimate=pl.CostEstimate(flops=0, bytes_accessed=6 * rows * pix, transcendentals=0),
        name="load_frames",
    )(*(pltpu.with_memory_space_constraint(x, pltpu.HBM) for x in (frames, orient, log_prior)))


def score_kernel(pieces, order, *refs):
    turned_ref, out_ref = refs[-2:]
    raw, squares = [], []
    for first, size, rows in pieces:
        model = jnp.concatenate([refs[order.index(ref)][:, pl.ds(column, size)] for ref, column in rows], axis=0)
        raw.append(jnp.dot(model, turned_ref[pl.ds(first, size), :], preferred_element_type=jnp.float32))
        wide = model.astype(jnp.float32)
        squares.append(tree_sum([jnp.square(wide[:, at : at + 128]) for at in range(0, wide.shape[1], 128)]))
        if len(raw) > 4:
            raw, squares = raw[1:4] + [raw[0] + raw[4]], squares[1:4] + [squares[0] + squares[4]]
    out_ref[...] = tree_sum(raw) - 0.5 * jnp.sum(tree_sum(squares), axis=1, keepdims=True)


def score_parts(blocks, pieces, many, turned):
    pix, rows = turned.shape
    order = GATHER_ORDER if len(blocks) > 1 else (0,)
    return pl.pallas_call(
        functools.partial(score_kernel, pieces, order),
        in_specs=[IN_VMEM] * (len(blocks) + 1),
        out_specs=IN_VMEM,
        out_shape=jax.ShapeDtypeStruct((many, rows), jnp.float32),
        compiler_params=params(),
        cost_estimate=pl.CostEstimate(flops=2 * rows * pix * many, bytes_accessed=2 * rows * pix, transcendentals=0),
        name="score_parts",
    )(*[blocks[i] for i in order], pltpu.with_memory_space_constraint(turned, pltpu.VMEM))


def gathered_pieces(pix, relayed):
    quarter = pix // 4
    half = quarter // 2
    pieces = []
    for part in range(2):
        for q in range(4):
            for at in range(0, half, math.gcd(half, 512)):
                there, here = q * quarter + part * half + at, q * half + at
                direct = part != relayed
                rows = [(0, there), (1, there), (2 + direct, here), (4 + direct, here)]
                pieces.append((there, math.gcd(half, 512), rows))
    return pieces


def weigh(parts, prior_ref):
    raw = tree_sum([ref[...] for ref in parts])
    scores = (3.0 / math.sqrt(PIX)) * raw + prior_ref[...]
    up = jnp.exp(scores - jnp.max(scores, axis=0, keepdims=True))
    weights = (up / jnp.sum(up, axis=0, keepdims=True)).astype(jnp.bfloat16).astype(jnp.float32)
    counts = jnp.sum(weights, axis=1, keepdims=True)
    high = counts.astype(jnp.bfloat16).astype(jnp.float32)
    lane = lax.broadcasted_iota(jnp.int32, (counts.shape[0], TAIL), 1)
    return weights, jnp.where(lane < TAIL // 2, high, counts - high)


def plain_totals_kernel(n, *refs):
    parts, prior_ref, frames_ref, out_ref = refs[:n], refs[n], refs[n + 1], refs[n + 2]
    weights, tail = weigh(parts, prior_ref)
    weights = weights.astype(jnp.bfloat16)
    pix = frames_ref.shape[1]
    for piece in chunks(pix, 512):
        total = jnp.dot(weights, frames_ref[:, piece], preferred_element_type=jnp.float32)
        out_ref[:, piece] = total.astype(jnp.bfloat16)
    out_ref[:, pix:] = tail.astype(jnp.bfloat16)


def dense_totals_kernel(n, *refs):
    parts, prior_ref, frames_ref, outs = refs[:n], refs[n], refs[n + 1], refs[n + 2 :]
    weights, tail = weigh(parts, prior_ref)
    quarter = frames_ref.shape[1] // 4
    half = quarter // 2
    for k, out_ref in enumerate([outs[0], outs[1], outs[3], outs[5]]):
        rows = jnp.concatenate([tail[4 * k : 4 * k + 4]] * 4, axis=0)
        out_ref[:, out_ref.shape[1] - TAIL :] = rows.astype(jnp.bfloat16)
    turned = [rotate_rows(weights, (-4 * q) % 16).astype(jnp.bfloat16) for q in range(4)]
    for part in range(2):
        for piece in chunks(half, 512):
            totals = [
                jnp.dot(
                    turned[q],
                    frames_ref[:, pl.ds(q * quarter + part * half + piece.start, piece.size)],
                    preferred_element_type=jnp.float32,
                )
                for q in range(4)
            ]
            upper = lax.broadcasted_iota(jnp.int32, (8, piece.size), 0) < 4
            whole = pl.ds(part * half + piece.start, piece.size)
            spots = [(outs[0], whole), (outs[1], whole), (outs[2 + part], piece), (outs[4 + part], piece)]
            for k, (out_ref, spot) in enumerate(spots):
                first = jnp.where(upper, totals[-k % 4][:8], totals[(1 - k) % 4][:8])
                second = jnp.where(upper, totals[(2 - k) % 4][8:], totals[(3 - k) % 4][8:])
                out_ref[:, spot] = jnp.concatenate([first, second], axis=0).astype(jnp.bfloat16)


def block_totals(parts, prior, frames, dense):
    rows, pix = frames.shape
    many = prior.shape[0]
    if dense:
        half = pix // 8
        kernel = dense_totals_kernel
        shapes = [(16, 2 * half + TAIL)] * 2 + [(16, half), (16, half + TAIL)] * 2
    else:
        kernel, shapes = plain_totals_kernel, [(many, pix + TAIL)]
    return pl.pallas_call(
        functools.partial(kernel, len(parts)),
        in_specs=[IN_VMEM] * (len(parts) + 2),
        out_specs=[IN_VMEM] * len(shapes),
        out_shape=[jax.ShapeDtypeStruct(shape, jnp.bfloat16) for shape in shapes],
        compiler_params=params(),
        cost_estimate=pl.CostEstimate(
            flops=2 * rows * pix * many, bytes_accessed=2 * rows * pix, transcendentals=rows * many
        ),
        name="block_totals",
    )(*parts, prior, pltpu.with_memory_space_constraint(frames, pltpu.VMEM))


def plain_update_kernel(terms_ref, owned_ref, out_ref):
    pix = owned_ref.shape[1]
    tail = jnp.sum(terms_ref[:, :, pix:].astype(jnp.float32), axis=0)
    counts = tail[:, :1] + tail[:, TAIL // 2 : TAIL // 2 + 1]
    for piece in chunks(pix, 512):
        total = jnp.sum(terms_ref[:, :, piece].astype(jnp.float32), axis=0)
        out_ref[:, piece] = ((total + owned_ref[:, piece].astype(jnp.float32)) / (counts + 1.0)).astype(out_ref.dtype)


def dense_update_kernel(parts, *refs):
    own_ref, near_ref, joined_ref, direct_2_ref, direct_3_ref, owned_ref = refs[:6]
    out_ref, half_refs = refs[-1], refs[-2:-1]
    if len(refs) < 8:
        half_refs = []
    quarter = owned_ref.shape[1] // 4
    half = quarter // 2

    def total(terms):
        return tree_sum([rotate_rows(ref[:, spot].astype(jnp.float32), 4 * k) for k, ref, spot in terms])

    behind, behind_half = pl.ds(quarter, TAIL), pl.ds(half, TAIL)
    tail = total(
        [(0, own_ref, behind), (1, near_ref, behind), (2, direct_2_ref, behind_half), (3, direct_3_ref, behind_half)]
    )
    scale = tail[:, :1] + tail[:, TAIL // 2 : TAIL // 2 + 1] + 1.0
    for part in parts:
        for piece in chunks(half, 512):
            whole = pl.ds(part * half + piece.start, piece.size)
            terms = [(0, own_ref, whole), (1, near_ref, whole)]
            terms += [(2, direct_2_ref, piece), (3, direct_3_ref, piece)] if part else [(2, joined_ref, piece)]
            spots = [pl.ds(q * quarter + whole.start, whole.size) for q in range(4)]
            owned = jnp.concatenate([owned_ref[:, spot].astype(jnp.float32) for spot in spots], axis=0)
            new = ((total(terms) + owned) / scale).astype(out_ref.dtype)
            for q, spot in enumerate(spots):
                out_ref[:, spot] = new[4 * q : 4 * q + 4]
                for half_ref in half_refs:
                    half_ref[:, pl.ds(q * half + piece.start, piece.size)] = new[4 * q : 4 * q + 4]


def update_call(kernel, operands, shapes, aliases={}):
    size = operands[0].size
    return pl.pallas_call(
        kernel,
        in_specs=[IN_VMEM] * len(operands),
        out_specs=[IN_VMEM] * len(shapes),
        out_shape=shapes,
        input_output_aliases=aliases,
        compiler_params=params(),
        cost_estimate=pl.CostEstimate(flops=8 * size, bytes_accessed=12 * size, transcendentals=0),
        name="update",
    )(*operands)


def update_in_parts(terms, owned):
    own, near, joined, direct_2, direct_3 = terms
    many, pix = owned.shape
    half, whole = (jax.ShapeDtypeStruct((many, size), jnp.bfloat16) for size in (pix // 2, pix))

    def second(own_ref, near_ref, direct_2_ref, direct_3_ref, owned_ref, *outs):
        dense_update_kernel((1,), own_ref, near_ref, None, direct_2_ref, direct_3_ref, owned_ref, *outs)

    def first(own_ref, near_ref, joined_ref, direct_2_ref, direct_3_ref, owned_ref, _, *outs):
        dense_update_kernel((0,), own_ref, near_ref, joined_ref, direct_2_ref, direct_3_ref, owned_ref, *outs)

    part_1, begun = update_call(second, (own, near, direct_2, direct_3, owned), [half, whole])
    part_0, done = update_call(first, (*terms, owned, begun), [half, whole], {6: 1})
    return [done, part_1, part_0]


def local(sizes, frames, slices, log_prior, orient):
    along, across = sizes
    owned, pix = slices.shape
    dense = along == 4 and owned == 4 and pix % 2048 == 0
    owned_b = round_slices(slices) if dense else [slices.astype(jnp.bfloat16)]
    if not dense:
        here, turned, prior = load_frames(frames, orient, log_prior, dense)
    for step in range(ITERS):
        last = step + 1 == ITERS
        if dense:
            blocks, over = gather_line(*owned_b)
            if step == 0:
                frames, over = lax.optimization_barrier((frames, over))
                here, turned, prior = load_frames(frames, orient, log_prior, dense)
            pieces = gathered_pieces(pix, step % 2)
        else:
            blocks = [lax.all_gather(owned_b[0], "frame", axis=0, tiled=True)]
            pieces = [(piece.start, piece.size, [(0, piece.start)]) for piece in chunks(pix, 512)]
        parts = exchange_all(
            score_parts(blocks, pieces, along * owned, turned), ("panel", "sub"), across
        )
        totals = block_totals(parts, prior, here, dense)
        if dense:
            terms = scatter_line(*totals)
        else:
            whole = totals[0].reshape(along, owned, totals[0].shape[1])
            terms = [lax.all_to_all(whole, "frame", split_axis=0, concat_axis=0, tiled=False)]
        if dense and not last:
            owned_b = update_in_parts(terms, owned_b[0])
        else:
            kernel = functools.partial(dense_update_kernel, (0, 1)) if dense else plain_update_kernel
            shape = jax.ShapeDtypeStruct(slices.shape, jnp.float32 if last else jnp.bfloat16)
            owned_b = update_call(kernel, (*terms, owned_b[0]), [shape])
    return owned_b[0]


def solution(mesh):
    in_specs = (
        P(("groups", "frame"), ("panel", "sub")),
        P(("groups", "frame"), ("panel", "sub")),
        P(),
        P("groups"),
    )
    out_specs = P(("groups", "frame"), ("panel", "sub"))
    sizes = (mesh.shape["frame"], mesh.shape["panel"] * mesh.shape["sub"])
    return jax.shard_map(
        functools.partial(local, sizes), mesh=mesh, in_specs=in_specs, out_specs=out_specs, check_vma=False
    )
```

```python
import functools
import math

import jax
import jax.numpy as jnp
from jax import lax
from jax.experimental import pallas as pl
from jax.experimental.pallas import tpu as pltpu
from jax.sharding import PartitionSpec as P

PIX = 65536
ITERS = 2
TAIL = 128
VMEM_BYTES = 12 * 1024 * 1024
IN_VMEM = pl.BlockSpec(memory_space=pltpu.VMEM)


def params():
    return pltpu.CompilerParams(vmem_limit_bytes=VMEM_BYTES)


def tree_sum(terms):
    while len(terms) > 1:
        terms = [a + b for a, b in zip(terms[::2], terms[1::2])] + terms[len(terms) & ~1 :]
    return terms[0]


def chunks(size, most):
    step = math.gcd(size, most)
    return [pl.ds(at, step) for at in range(0, size, step)]


def rotate_rows(value, by):
    return value if by == 0 else jnp.concatenate([value[by:], value[:by]], axis=0)


def early(value, flops):
    return pl.pallas_call(
        lambda in_ref, out_ref: None,
        in_specs=[pl.BlockSpec(memory_space=pl.ANY)],
        out_specs=pl.BlockSpec(memory_space=pl.ANY),
        out_shape=jax.ShapeDtypeStruct(value.shape, value.dtype),
        input_output_aliases={0: 0},
        compiler_params=params(),
        cost_estimate=pl.CostEstimate(flops=flops, bytes_accessed=0, transcendentals=0),
        name="early",
    )(value)


def swap(value, distance):
    return lax.ppermute(value, "frame", [(i, i ^ distance) for i in range(4)])


def gather_line(whole, relayed, direct):
    over = swap(relayed, 2)
    direct_2 = swap(direct, 2)
    direct_3 = swap(direct, 3)
    near = swap(whole, 1)
    return [whole, near, over, direct_2, swap(over, 1), direct_3], over


def round_kernel(slices_ref, whole_ref, first_ref, second_ref, held_ref, sems):
    pix = slices_ref.shape[1]
    quarter, half = pix // 4, pix // 8
    copies = [
        pltpu.make_async_copy(
            slices_ref.at[:, pl.ds(q * quarter, quarter)], held_ref.at[:, pl.ds(q * quarter, quarter)], sems.at[q]
        )
        for q in range(4)
    ]
    for copy in copies:
        copy.start()
    for q, copy in enumerate(copies):
        copy.wait()
        for part, out_ref in enumerate((first_ref, second_ref)):
            there = pl.ds(q * quarter + part * half, half)
            value = held_ref[:, there].astype(jnp.bfloat16)
            whole_ref[:, there] = value
            out_ref[:, pl.ds(q * half, half)] = value


def round_slices(slices):
    owned, pix = slices.shape
    return pl.pallas_call(
        round_kernel,
        in_specs=[pl.BlockSpec(memory_space=pl.ANY)],
        out_specs=[IN_VMEM] * 3,
        out_shape=[jax.ShapeDtypeStruct((owned, size), jnp.bfloat16) for size in (pix, pix // 2, pix // 2)],
        scratch_shapes=[pltpu.VMEM((owned, pix), slices.dtype), pltpu.SemaphoreType.DMA((4,))],
        compiler_params=params(),
        cost_estimate=pl.CostEstimate(flops=5 * 10**9, bytes_accessed=8 * slices.size, transcendentals=0),
        name="round_slices",
    )(pltpu.with_memory_space_constraint(slices, pltpu.HBM))


def relay_kernel(came_ref, own_ref, out_ref):
    for piece in chunks(own_ref.shape[1], 512):
        came = rotate_rows(came_ref[:, piece].astype(jnp.float32), 4)
        out_ref[:, piece] = (came + own_ref[:, piece].astype(jnp.float32)).astype(jnp.bfloat16)


def scatter_line(own, *others):
    *near, relayed_2, direct_2, relayed_3, direct_3 = others
    came = swap(relayed_3, 1)
    joined = pl.pallas_call(
        relay_kernel,
        in_specs=[IN_VMEM] * 2,
        out_specs=IN_VMEM,
        out_shape=jax.ShapeDtypeStruct(came.shape, came.dtype),
        compiler_params=params(),
        cost_estimate=pl.CostEstimate(flops=2 * came.size, bytes_accessed=6 * came.size, transcendentals=0),
        name="relay",
    )(came, relayed_2)
    joined = swap(joined, 2)
    direct_3 = early(swap(direct_3, 3), 10**9)
    direct_2 = early(swap(direct_2, 2), 10**9)
    if len(near) > 1:
        direct_2, near_0 = lax.optimization_barrier((direct_2, near[0]))
        near = [swap(near_0, 1), swap(near[1], 1)]
    else:
        near = [swap(near[0], 1)]
    return [own, near, joined, direct_2, direct_3]


def exchange_all(part, axes, size):
    if size & (size - 1):
        return [lax.psum(part, axes)]
    return [part] + [lax.ppermute(part, axes, [(i, i ^ k) for i in range(size)]) for k in range(1, size)]


def load_kernel(dense, here_ref, orient_in_ref, log_prior_in_ref, turned_ref, prior_ref, orient_ref, log_prior_ref, sems):
    tables = [
        pltpu.make_async_copy(orient_in_ref, orient_ref, sems.at[0]),
        pltpu.make_async_copy(log_prior_in_ref, log_prior_ref, sems.at[1]),
    ]
    for copy in tables:
        copy.start()
    for piece in chunks(here_ref.shape[1], 512):
        turned_ref[piece, :] = here_ref[:, piece].T
    for table in tables:
        table.wait()
    many, columns = prior_ref.shape
    place = lax.axis_index("frame")
    for row in range(many):
        spot = 4 * (place ^ (row // 4)) + row % 4 if dense else row
        prior_ref[row : row + 1, :] = jnp.full((1, columns), log_prior_ref[orient_ref[spot]], jnp.float32)


def load_frames(frames, orient, log_prior, dense):
    rows, pix = frames.shape
    here = pltpu.with_memory_space_constraint(frames, pltpu.VMEM)
    turned, prior = pl.pallas_call(
        functools.partial(load_kernel, dense),
        in_specs=[IN_VMEM] + [pl.BlockSpec(memory_space=pl.ANY)] * 2,
        out_specs=[IN_VMEM] * 2,
        out_shape=[
            pltpu.VMEM((pix, rows), frames.dtype),
            jax.ShapeDtypeStruct((orient.shape[0], rows), jnp.float32),
        ],
        scratch_shapes=[
            pltpu.SMEM(orient.shape, orient.dtype),
            pltpu.SMEM(log_prior.shape, log_prior.dtype),
            pltpu.SemaphoreType.DMA((2,)),
        ],
        compiler_params=params(),
        cost_estimate=pl.CostEstimate(flops=0, bytes_accessed=6 * rows * pix, transcendentals=0),
        name="load_frames",
    )(here, *(pltpu.with_memory_space_constraint(x, pltpu.HBM) for x in (orient, log_prior)))
    return frames, turned, prior


def score_kernel(pieces, *refs):
    turned_ref, out_ref = refs[-2:]
    raw, squares = [], []
    for first, size, rows in pieces:
        model = jnp.concatenate([refs[ref][:, pl.ds(column, size)] for ref, column in rows], axis=0)
        raw.append(jnp.dot(model, turned_ref[pl.ds(first, size), :], preferred_element_type=jnp.float32))
        wide = model.astype(jnp.float32)
        squares.append(tree_sum([jnp.square(wide[:, at : at + 128]) for at in range(0, wide.shape[1], 128)]))
        if len(raw) > 4:
            raw, squares = raw[1:4] + [raw[0] + raw[4]], squares[1:4] + [squares[0] + squares[4]]
    out_ref[...] = tree_sum(raw) - 0.5 * jnp.sum(tree_sum(squares), axis=1, keepdims=True)


def score_parts(blocks, pieces, many, turned):
    pix, rows = turned.shape
    return pl.pallas_call(
        functools.partial(score_kernel, pieces),
        in_specs=[IN_VMEM] * (len(blocks) + 1),
        out_specs=IN_VMEM,
        out_shape=jax.ShapeDtypeStruct((many, rows), jnp.float32),
        compiler_params=params(),
        cost_estimate=pl.CostEstimate(flops=2 * rows * pix * many, bytes_accessed=2 * rows * pix, transcendentals=0),
        name="score_parts",
    )(*blocks, pltpu.with_memory_space_constraint(turned, pltpu.VMEM))


def gathered_pieces(pix, relayed):
    quarter = pix // 4
    half = quarter // 2
    pieces = []
    for part in range(2):
        for q in range(4):
            for at in range(0, half, math.gcd(half, 512)):
                there, here = q * quarter + part * half + at, q * half + at
                direct = part != relayed
                rows = [(0, there), (1, there), (2 + direct, here), (4 + direct, here)]
                pieces.append((there, math.gcd(half, 512), rows))
    return pieces


def weigh(parts, prior_ref):
    raw = tree_sum([ref[...] for ref in parts])
    scores = (3.0 / math.sqrt(PIX)) * raw + prior_ref[...]
    up = jnp.exp(scores - jnp.max(scores, axis=0, keepdims=True))
    weights = (up / jnp.sum(up, axis=0, keepdims=True)).astype(jnp.bfloat16).astype(jnp.float32)
    counts = jnp.sum(weights, axis=1, keepdims=True)
    high = counts.astype(jnp.bfloat16).astype(jnp.float32)
    lane = lax.broadcasted_iota(jnp.int32, (counts.shape[0], TAIL), 1)
    return weights, jnp.where(lane < TAIL // 2, high, counts - high)


def plain_totals_kernel(n, *refs):
    parts, prior_ref, frames_ref, out_ref = refs[:n], refs[n], refs[n + 1], refs[n + 2]
    weights, tail = weigh(parts, prior_ref)
    weights = weights.astype(jnp.bfloat16)
    pix = frames_ref.shape[1]
    for piece in chunks(pix, 512):
        total = jnp.dot(weights, frames_ref[:, piece], preferred_element_type=jnp.float32)
        out_ref[:, piece] = total.astype(jnp.bfloat16)
    out_ref[:, pix:] = tail.astype(jnp.bfloat16)


def dense_totals_kernel(n, *refs):
    parts, prior_ref, frames_ref, outs = refs[:n], refs[n], refs[n + 1], refs[n + 2 :]
    weights, tail = weigh(parts, prior_ref)
    quarter = frames_ref.shape[1] // 4
    half = quarter // 2
    own_ref, *near_refs = outs[:-4]
    two_refs, three_refs = outs[-4:-2], outs[-2:]
    for k, out_ref in enumerate([own_ref, near_refs[-1], two_refs[1], three_refs[1]]):
        rows = jnp.concatenate([tail[4 * k : 4 * k + 4]] * 4, axis=0)
        out_ref[:, out_ref.shape[1] - TAIL :] = rows.astype(jnp.bfloat16)
    turned = [rotate_rows(weights, (-4 * q) % 16).astype(jnp.bfloat16) for q in range(4)]
    for part in range(2):
        for piece in chunks(half, 512):
            totals = [
                jnp.dot(
                    turned[q],
                    frames_ref[:, pl.ds(q * quarter + part * half + piece.start, piece.size)],
                    preferred_element_type=jnp.float32,
                )
                for q in range(4)
            ]
            upper = lax.broadcasted_iota(jnp.int32, (8, piece.size), 0) < 4
            whole = pl.ds(part * half + piece.start, piece.size)
            near = (near_refs[part], piece) if len(near_refs) > 1 else (near_refs[0], whole)
            spots = [(own_ref, whole), near, (two_refs[part], piece), (three_refs[part], piece)]
            for k, (out_ref, spot) in enumerate(spots):
                first = jnp.where(upper, totals[-k % 4][:8], totals[(1 - k) % 4][:8])
                second = jnp.where(upper, totals[(2 - k) % 4][8:], totals[(3 - k) % 4][8:])
                out_ref[:, spot] = jnp.concatenate([first, second], axis=0).astype(jnp.bfloat16)


def block_totals(parts, prior, frames, dense, near_halves):
    rows, pix = frames.shape
    many = prior.shape[0]
    if dense:
        half = pix // 8
        kernel = dense_totals_kernel
        whole, halves = [(16, 2 * half + TAIL)], [(16, half), (16, half + TAIL)]
        shapes = whole + (halves if near_halves else whole) + 2 * halves
    else:
        kernel, shapes = plain_totals_kernel, [(many, pix + TAIL)]
    return pl.pallas_call(
        functools.partial(kernel, len(parts)),
        in_specs=[IN_VMEM] * (len(parts) + 2),
        out_specs=[IN_VMEM] * len(shapes),
        out_shape=[jax.ShapeDtypeStruct(shape, jnp.bfloat16) for shape in shapes],
        compiler_params=params(),
        cost_estimate=pl.CostEstimate(
            flops=2 * rows * pix * many, bytes_accessed=2 * rows * pix, transcendentals=rows * many
        ),
        name="block_totals",
    )(*parts, prior, pltpu.with_memory_space_constraint(frames, pltpu.VMEM))


def plain_update_kernel(terms_ref, owned_ref, out_ref):
    pix = owned_ref.shape[1]
    tail = jnp.sum(terms_ref[:, :, pix:].astype(jnp.float32), axis=0)
    counts = tail[:, :1] + tail[:, TAIL // 2 : TAIL // 2 + 1]
    for piece in chunks(pix, 512):
        total = jnp.sum(terms_ref[:, :, piece].astype(jnp.float32), axis=0)
        out_ref[:, piece] = ((total + owned_ref[:, piece].astype(jnp.float32)) / (counts + 1.0)).astype(out_ref.dtype)


def dense_update_kernel(parts, *refs):
    own_ref, near_refs, joined_ref, direct_2_ref, direct_3_ref, owned_ref = refs[:6]
    out_ref, half_refs = refs[-1], refs[-2:-1]
    if len(refs) < 8:
        half_refs = []
    quarter = owned_ref.shape[1] // 4
    half = quarter // 2

    def total(terms):
        return tree_sum([rotate_rows(ref[:, spot].astype(jnp.float32), 4 * k) for k, ref, spot in terms])

    behind, behind_half = pl.ds(quarter, TAIL), pl.ds(half, TAIL)
    tail = total(
        [
            (0, own_ref, behind),
            (1, near_refs[-1], behind_half if len(near_refs) > 1 else behind),
            (2, direct_2_ref, behind_half),
            (3, direct_3_ref, behind_half),
        ]
    )
    scale = tail[:, :1] + tail[:, TAIL // 2 : TAIL // 2 + 1] + 1.0
    for part in parts:
        for piece in chunks(half, 512):
            whole = pl.ds(part * half + piece.start, piece.size)
            terms = [(0, own_ref, whole)]
            terms += [(1, near_refs[part], piece) if len(near_refs) > 1 else (1, near_refs[0], whole)]
            terms += [(2, direct_2_ref, piece), (3, direct_3_ref, piece)] if part else [(2, joined_ref, piece)]
            spots = [pl.ds(q * quarter + whole.start, whole.size) for q in range(4)]
            owned = jnp.concatenate([owned_ref[:, spot].astype(jnp.float32) for spot in spots], axis=0)
            new = ((total(terms) + owned) / scale).astype(out_ref.dtype)
            for q, spot in enumerate(spots):
                out_ref[:, spot] = new[4 * q : 4 * q + 4]
                for half_ref in half_refs:
                    half_ref[:, pl.ds(q * half + piece.start, piece.size)] = new[4 * q : 4 * q + 4]


def last_update_kernel(own_ref, near_ref, *refs):
    dense_update_kernel((0, 1), own_ref, (near_ref,), *refs)


def update_call(kernel, operands, shapes, aliases={}):
    size = operands[0].size
    return pl.pallas_call(
        kernel,
        in_specs=[IN_VMEM] * len(operands),
        out_specs=[IN_VMEM] * len(shapes),
        out_shape=shapes,
        input_output_aliases=aliases,
        compiler_params=params(),
        cost_estimate=pl.CostEstimate(flops=8 * size, bytes_accessed=12 * size, transcendentals=0),
        name="update",
    )(*operands)


def update_in_parts(terms, owned):
    own, near, joined, direct_2, direct_3 = terms
    many, pix = owned.shape
    half, whole = (jax.ShapeDtypeStruct((many, size), jnp.bfloat16) for size in (pix // 2, pix))

    def second(own_ref, near_1_ref, direct_2_ref, direct_3_ref, owned_ref, *outs):
        dense_update_kernel((1,), own_ref, (None, near_1_ref), None, direct_2_ref, direct_3_ref, owned_ref, *outs)

    def first(own_ref, near_0_ref, near_1_ref, joined_ref, direct_2_ref, direct_3_ref, owned_ref, _, *outs):
        near_refs = (near_0_ref, near_1_ref)
        dense_update_kernel((0,), own_ref, near_refs, joined_ref, direct_2_ref, direct_3_ref, owned_ref, *outs)

    part_1, begun = update_call(second, (own, near[1], direct_2, direct_3, owned), [half, whole])
    operands = (own, *near, joined, direct_2, direct_3, owned, begun)
    part_0, done = update_call(first, operands, [half, whole], {7: 1})
    return [done, part_1, part_0]


def local(sizes, frames, slices, log_prior, orient):
    along, across = sizes
    owned, pix = slices.shape
    dense = along == 4 and owned == 4 and pix % 2048 == 0
    owned_b = round_slices(slices) if dense else [slices.astype(jnp.bfloat16)]
    if not dense:
        here, turned, prior = load_frames(frames, orient, log_prior, dense)
    for step in range(ITERS):
        last = step + 1 == ITERS
        if dense:
            blocks, over = gather_line(*owned_b)
            if step == 0:
                frames, over = lax.optimization_barrier((frames, over))
                here, turned, prior = load_frames(frames, orient, log_prior, dense)
            pieces = gathered_pieces(pix, step % 2)
        else:
            blocks = [lax.all_gather(owned_b[0], "frame", axis=0, tiled=True)]
            pieces = [(piece.start, piece.size, [(0, piece.start)]) for piece in chunks(pix, 512)]
        parts = exchange_all(
            score_parts(blocks, pieces, along * owned, turned), ("panel", "sub"), across
        )
        totals = block_totals(parts, prior, here, dense, not last)
        if dense:
            terms = scatter_line(*totals)
        else:
            whole = totals[0].reshape(along, owned, totals[0].shape[1])
            terms = [lax.all_to_all(whole, "frame", split_axis=0, concat_axis=0, tiled=False)]
        if dense and not last:
            owned_b = update_in_parts(terms, owned_b[0])
        else:
            kernel = last_update_kernel if dense else plain_update_kernel
            if dense:
                terms[1:2] = terms[1]
            shape = jax.ShapeDtypeStruct(slices.shape, jnp.float32 if last else jnp.bfloat16)
            owned_b = update_call(kernel, (*terms, owned_b[0]), [shape])
    return owned_b[0]


def solution(mesh):
    in_specs = (
        P(("groups", "frame"), ("panel", "sub")),
        P(("groups", "frame"), ("panel", "sub")),
        P(),
        P("groups"),
    )
    out_specs = P(("groups", "frame"), ("panel", "sub"))
    sizes = (mesh.shape["frame"], mesh.shape["panel"] * mesh.shape["sub"])
    return jax.shard_map(
        functools.partial(local, sizes), mesh=mesh, in_specs=in_specs, out_specs=out_specs, check_vma=False
    )
```

```python
import functools
import math

import jax
import jax.numpy as jnp
from jax import lax
from jax.experimental import pallas as pl
from jax.experimental.pallas import tpu as pltpu
from jax.sharding import PartitionSpec as P

PIX = 65536
ITERS = 2
LEAD = 1
TAIL = 128
VMEM_BYTES = 12 * 1024 * 1024
IN_VMEM = pl.BlockSpec(memory_space=pltpu.VMEM)


def params():
    return pltpu.CompilerParams(vmem_limit_bytes=VMEM_BYTES)


def tree_sum(terms):
    while len(terms) > 1:
        terms = [a + b for a, b in zip(terms[::2], terms[1::2])] + terms[len(terms) & ~1 :]
    return terms[0]


def chunks(size, most):
    step = math.gcd(size, most)
    return [pl.ds(at, step) for at in range(0, size, step)]


def rotate_rows(value, by):
    return value if by == 0 else jnp.concatenate([value[by:], value[:by]], axis=0)


def early(value, flops):
    return pl.pallas_call(
        lambda in_ref, out_ref: None,
        in_specs=[pl.BlockSpec(memory_space=pl.ANY)],
        out_specs=pl.BlockSpec(memory_space=pl.ANY),
        out_shape=jax.ShapeDtypeStruct(value.shape, value.dtype),
        input_output_aliases={0: 0},
        compiler_params=params(),
        cost_estimate=pl.CostEstimate(flops=flops, bytes_accessed=0, transcendentals=0),
        name="early",
    )(value)


def swap(value, distance):
    return lax.ppermute(value, "frame", [(i, i ^ distance) for i in range(4)])


def gather_line(whole, relayed, direct):
    over = swap(relayed, 2)
    direct_2 = swap(direct, 2)
    direct_3 = swap(direct, 3)
    near = swap(whole, 1)
    return [whole, near, over, direct_2, swap(over, 1), direct_3], over


def round_kernel(slices_ref, whole_ref, first_ref, second_ref, held_ref, sems):
    pix = slices_ref.shape[1]
    quarter, half = pix // 4, pix // 8
    copies = [
        pltpu.make_async_copy(
            slices_ref.at[:, pl.ds(q * quarter, quarter)], held_ref.at[:, pl.ds(q * quarter, quarter)], sems.at[q]
        )
        for q in range(4)
    ]
    for copy in copies:
        copy.start()
    for q, copy in enumerate(copies):
        copy.wait()
        for part, out_ref in enumerate((first_ref, second_ref)):
            there = pl.ds(q * quarter + part * half, half)
            value = held_ref[:, there].astype(jnp.bfloat16)
            whole_ref[:, there] = value
            out_ref[:, pl.ds(q * half, half)] = value


def round_slices(slices):
    owned, pix = slices.shape
    return pl.pallas_call(
        round_kernel,
        in_specs=[pl.BlockSpec(memory_space=pl.ANY)],
        out_specs=[IN_VMEM] * 3,
        out_shape=[jax.ShapeDtypeStruct((owned, size), jnp.bfloat16) for size in (pix, pix // 2, pix // 2)],
        scratch_shapes=[pltpu.VMEM((owned, pix), slices.dtype), pltpu.SemaphoreType.DMA((4,))],
        compiler_params=params(),
        cost_estimate=pl.CostEstimate(flops=5 * 10**9, bytes_accessed=8 * slices.size, transcendentals=0),
        name="round_slices",
    )(pltpu.with_memory_space_constraint(slices, pltpu.HBM))


def relay_kernel(came_ref, own_ref, out_ref):
    for piece in chunks(own_ref.shape[1], 512):
        came = rotate_rows(came_ref[:, piece].astype(jnp.float32), 4)
        out_ref[:, piece] = (came + own_ref[:, piece].astype(jnp.float32)).astype(jnp.bfloat16)


def scatter_line(own, *others):
    *near, relayed_2, direct_2, relayed_3, direct_3 = others
    came = swap(relayed_3, 1)
    joined = pl.pallas_call(
        relay_kernel,
        in_specs=[IN_VMEM] * 2,
        out_specs=IN_VMEM,
        out_shape=jax.ShapeDtypeStruct(came.shape, came.dtype),
        compiler_params=params(),
        cost_estimate=pl.CostEstimate(flops=2 * came.size, bytes_accessed=6 * came.size, transcendentals=0),
        name="relay",
    )(came, relayed_2)
    joined = swap(joined, 2)
    direct_3 = early(swap(direct_3, 3), 10**9)
    direct_2 = early(swap(direct_2, 2), 10**9)
    if len(near) > 1:
        direct_2, near_0 = lax.optimization_barrier((direct_2, near[0]))
        near = [swap(near_0, 1), swap(near[1], 1)]
    else:
        near = [swap(near[0], 1)]
    return [own, near, joined, direct_2, direct_3]


def exchange_all(part, axes, size):
    if size & (size - 1):
        return [lax.psum(part, axes)]
    return [part] + [lax.ppermute(part, axes, [(i, i ^ k) for i in range(size)]) for k in range(1, size)]


def load_kernel(dense, here_ref, orient_in_ref, log_prior_in_ref, turned_ref, prior_ref, orient_ref, log_prior_ref, sems):
    tables = [
        pltpu.make_async_copy(orient_in_ref, orient_ref, sems.at[0]),
        pltpu.make_async_copy(log_prior_in_ref, log_prior_ref, sems.at[1]),
    ]
    for copy in tables:
        copy.start()
    for piece in chunks(here_ref.shape[1], 512):
        turned_ref[piece, :] = here_ref[:, piece].T
    for table in tables:
        table.wait()
    many, columns = prior_ref.shape
    place = lax.axis_index("frame")
    for row in range(many):
        spot = 4 * (place ^ (row // 4)) + row % 4 if dense else row
        prior_ref[row : row + 1, :] = jnp.full((1, columns), log_prior_ref[orient_ref[spot]], jnp.float32)


def load_frames(frames, orient, log_prior, dense):
    rows, pix = frames.shape
    here = pltpu.with_memory_space_constraint(frames, pltpu.VMEM)
    turned, prior = pl.pallas_call(
        functools.partial(load_kernel, dense),
        in_specs=[IN_VMEM] + [pl.BlockSpec(memory_space=pl.ANY)] * 2,
        out_specs=[IN_VMEM] * 2,
        out_shape=[
            pltpu.VMEM((pix, rows), frames.dtype),
            jax.ShapeDtypeStruct((orient.shape[0], rows), jnp.float32),
        ],
        scratch_shapes=[
            pltpu.SMEM(orient.shape, orient.dtype),
            pltpu.SMEM(log_prior.shape, log_prior.dtype),
            pltpu.SemaphoreType.DMA((2,)),
        ],
        compiler_params=params(),
        cost_estimate=pl.CostEstimate(flops=0, bytes_accessed=6 * rows * pix, transcendentals=0),
        name="load_frames",
    )(here, *(pltpu.with_memory_space_constraint(x, pltpu.HBM) for x in (orient, log_prior)))
    return frames, turned, prior


def score_kernel(pieces, *refs):
    turned_ref, out_ref = refs[-2:]
    raw, squares = [], []
    for first, size, rows in pieces:
        model = jnp.concatenate([refs[ref][:, pl.ds(column, size)] for ref, column in rows], axis=0)
        raw.append(jnp.dot(model, turned_ref[pl.ds(first, size), :], preferred_element_type=jnp.float32))
        wide = model.astype(jnp.float32)
        squares.append(tree_sum([jnp.square(wide[:, at : at + 128]) for at in range(0, wide.shape[1], 128)]))
        if len(raw) > 4:
            raw, squares = raw[1:4] + [raw[0] + raw[4]], squares[1:4] + [squares[0] + squares[4]]
    out_ref[...] = tree_sum(raw) - 0.5 * jnp.sum(tree_sum(squares), axis=1, keepdims=True)


def score_parts(blocks, pieces, many, turned):
    pix, rows = turned.shape
    return pl.pallas_call(
        functools.partial(score_kernel, pieces),
        in_specs=[IN_VMEM] * (len(blocks) + 1),
        out_specs=IN_VMEM,
        out_shape=jax.ShapeDtypeStruct((many, rows), jnp.float32),
        compiler_params=params(),
        cost_estimate=pl.CostEstimate(flops=2 * rows * pix * many, bytes_accessed=2 * rows * pix, transcendentals=0),
        name="score_parts",
    )(*blocks, pltpu.with_memory_space_constraint(turned, pltpu.VMEM))


def gathered_pieces(pix, relayed):
    quarter = pix // 4
    half = quarter // 2
    pieces = []
    for part in range(2):
        for q in range(4):
            for at in range(0, half, math.gcd(half, 512)):
                there, here = q * quarter + part * half + at, q * half + at
                direct = part != relayed
                rows = [(0, there), (1, there), (2 + direct, here), (4 + direct, here)]
                pieces.append((there, math.gcd(half, 512), rows))
    return pieces


def split(counts):
    high = counts.astype(jnp.bfloat16).astype(jnp.float32)
    lane = lax.broadcasted_iota(jnp.int32, (counts.shape[0], TAIL), 1)
    return jnp.where(lane < TAIL // 2, high, counts - high)


def weigh(parts, prior_ref):
    raw = tree_sum([ref[...] for ref in parts])
    scores = (3.0 / math.sqrt(PIX)) * raw + prior_ref[...]
    up = jnp.exp(scores - jnp.max(scores, axis=0, keepdims=True))
    weights = (up / jnp.sum(up, axis=0, keepdims=True)).astype(jnp.bfloat16).astype(jnp.float32)
    counts = jnp.sum(weights, axis=1, keepdims=True)
    return weights, split(counts)


def plain_totals_kernel(n, *refs):
    parts, prior_ref, frames_ref, out_ref = refs[:n], refs[n], refs[n + 1], refs[n + 2]
    weights, tail = weigh(parts, prior_ref)
    weights = weights.astype(jnp.bfloat16)
    pix = frames_ref.shape[1]
    for piece in chunks(pix, 512):
        total = jnp.dot(weights, frames_ref[:, piece], preferred_element_type=jnp.float32)
        out_ref[:, piece] = total.astype(jnp.bfloat16)
    out_ref[:, pix:] = tail.astype(jnp.bfloat16)


def dense_totals_kernel(part, weights, frames_ref, own_ref, near_ref, two_ref, three_ref):
    quarter = frames_ref.shape[1] // 4
    half = quarter // 2
    turned = [rotate_rows(weights, (-4 * q) % 16).astype(jnp.bfloat16) for q in range(4)]
    for piece in chunks(half, 512):
        totals = [
            jnp.dot(
                turned[q],
                frames_ref[:, pl.ds(q * quarter + part * half + piece.start, piece.size)],
                preferred_element_type=jnp.float32,
            )
            for q in range(4)
        ]
        upper = lax.broadcasted_iota(jnp.int32, (8, piece.size), 0) < 4
        whole = pl.ds(part * half + piece.start, piece.size)
        near = whole if near_ref.shape[1] > quarter else piece
        spots = [(own_ref, whole), (near_ref, near), (two_ref, piece), (three_ref, piece)]
        for k, (out_ref, spot) in enumerate(spots):
            first = jnp.where(upper, totals[-k % 4][:8], totals[(1 - k) % 4][:8])
            second = jnp.where(upper, totals[(2 - k) % 4][8:], totals[(3 - k) % 4][8:])
            out_ref[:, spot] = jnp.concatenate([first, second], axis=0).astype(jnp.bfloat16)


def put_counts(tail, outs):
    for k, out_ref in outs:
        rows = jnp.concatenate([tail[4 * k : 4 * k + 4]] * 4, axis=0)
        out_ref[:, out_ref.shape[1] - TAIL :] = rows.astype(jnp.bfloat16)


def whole_totals_kernel(n, *refs):
    parts, prior_ref, frames_ref = refs[:n], refs[n], refs[n + 1]
    own_ref, near_0_ref, near_1_ref, two_0_ref, two_1_ref, three_0_ref, three_1_ref = refs[n + 2 :]
    weights, tail = weigh(parts, prior_ref)
    put_counts(tail, ((0, own_ref), (1, near_1_ref), (2, two_1_ref), (3, three_1_ref)))
    dense_totals_kernel(0, weights, frames_ref, own_ref, near_0_ref, two_0_ref, three_0_ref)
    dense_totals_kernel(1, weights, frames_ref, own_ref, near_1_ref, two_1_ref, three_1_ref)


def first_totals_kernel(n, part, *refs):
    parts, prior_ref, frames_ref, outs, weights_ref = refs[:n], refs[n], refs[n + 1], refs[n + 2 : n + 6], refs[n + 6]
    weights, tail = weigh(parts, prior_ref)
    weights_ref[...] = weights
    put_counts(tail, list(enumerate(outs)) if part else list(enumerate(outs[:2])))
    dense_totals_kernel(part, weights, frames_ref, *outs)


def second_totals_kernel(part, weights_ref, frames_ref, _own_ref, _near_ref, *outs):
    weights = weights_ref[...]
    if part:
        put_counts(split(jnp.sum(weights, axis=1, keepdims=True)), ((2, outs[2]), (3, outs[3])))
    dense_totals_kernel(part, weights, frames_ref, *outs)


def totals_call(kernel, operands, shapes, frames, aliases={}):
    rows, pix = frames.shape
    many = 16
    return pl.pallas_call(
        kernel,
        in_specs=[IN_VMEM] * len(operands),
        out_specs=[IN_VMEM] * len(shapes),
        out_shape=shapes,
        input_output_aliases=aliases,
        compiler_params=params(),
        cost_estimate=pl.CostEstimate(
            flops=rows * pix * many, bytes_accessed=rows * pix, transcendentals=rows * many
        ),
        name="block_totals",
    )(*operands)


def block_totals(parts, prior, frames, dense, near_halves):
    rows, pix = frames.shape
    many = prior.shape[0]
    frames = pltpu.with_memory_space_constraint(frames, pltpu.VMEM)
    if not dense:
        whole = jax.ShapeDtypeStruct((many, pix + TAIL), jnp.bfloat16)
        return totals_call(
            functools.partial(plain_totals_kernel, len(parts)), (*parts, prior, frames), [whole], frames
        )
    whole, half, half_tail = (
        jax.ShapeDtypeStruct((16, size), jnp.bfloat16) for size in (pix // 4 + TAIL, pix // 8, pix // 8 + TAIL)
    )
    if near_halves:
        return totals_call(
            functools.partial(whole_totals_kernel, len(parts)),
            (*parts, prior, frames),
            [whole, half, half_tail, half, half_tail, half, half_tail],
            frames,
        )
    sizes = (half, half_tail)
    own, near, two, three, weights = totals_call(
        functools.partial(first_totals_kernel, len(parts), LEAD),
        (*parts, prior, frames),
        [whole, whole, sizes[LEAD], sizes[LEAD], jax.ShapeDtypeStruct((many, rows), jnp.float32)],
        frames,
    )
    own, near, *other = totals_call(
        functools.partial(second_totals_kernel, 1 - LEAD),
        (weights, frames, own, near),
        [whole, whole, sizes[1 - LEAD], sizes[1 - LEAD]],
        frames,
        {2: 0, 3: 1},
    )
    twos, threes = (two, other[0]), (three, other[1])
    return own, near, twos[LEAD], twos[1 - LEAD], threes[LEAD], threes[1 - LEAD]


def plain_update_kernel(terms_ref, owned_ref, out_ref):
    pix = owned_ref.shape[1]
    tail = jnp.sum(terms_ref[:, :, pix:].astype(jnp.float32), axis=0)
    counts = tail[:, :1] + tail[:, TAIL // 2 : TAIL // 2 + 1]
    for piece in chunks(pix, 512):
        total = jnp.sum(terms_ref[:, :, piece].astype(jnp.float32), axis=0)
        out_ref[:, piece] = ((total + owned_ref[:, piece].astype(jnp.float32)) / (counts + 1.0)).astype(out_ref.dtype)


def dense_update_kernel(parts, *refs):
    own_ref, near_refs, joined_ref, direct_2_ref, direct_3_ref, owned_ref = refs[:6]
    out_ref, half_refs = refs[-1], refs[-2:-1]
    if len(refs) < 8:
        half_refs = []
    quarter = owned_ref.shape[1] // 4
    half = quarter // 2

    def total(terms):
        return tree_sum([rotate_rows(ref[:, spot].astype(jnp.float32), 4 * k) for k, ref, spot in terms])

    behind, behind_half = pl.ds(quarter, TAIL), pl.ds(half, TAIL)
    tail = total(
        [
            (0, own_ref, behind),
            (1, near_refs[-1], behind_half if len(near_refs) > 1 else behind),
            (2, direct_2_ref, behind_half),
            (3, direct_3_ref, behind_half),
        ]
    )
    scale = tail[:, :1] + tail[:, TAIL // 2 : TAIL // 2 + 1] + 1.0
    for part in parts:
        for piece in chunks(half, 512):
            whole = pl.ds(part * half + piece.start, piece.size)
            terms = [(0, own_ref, whole)]
            terms += [(1, near_refs[part], piece) if len(near_refs) > 1 else (1, near_refs[0], whole)]
            terms += [(2, direct_2_ref, piece), (3, direct_3_ref, piece)] if part else [(2, joined_ref, piece)]
            spots = [pl.ds(q * quarter + whole.start, whole.size) for q in range(4)]
            owned = jnp.concatenate([owned_ref[:, spot].astype(jnp.float32) for spot in spots], axis=0)
            new = ((total(terms) + owned) / scale).astype(out_ref.dtype)
            for q, spot in enumerate(spots):
                out_ref[:, spot] = new[4 * q : 4 * q + 4]
                for half_ref in half_refs:
                    half_ref[:, pl.ds(q * half + piece.start, piece.size)] = new[4 * q : 4 * q + 4]


def last_update_kernel(own_ref, near_ref, *refs):
    dense_update_kernel((0, 1), own_ref, (near_ref,), *refs)


def update_call(kernel, operands, shapes, aliases={}):
    size = operands[0].size
    return pl.pallas_call(
        kernel,
        in_specs=[IN_VMEM] * len(operands),
        out_specs=[IN_VMEM] * len(shapes),
        out_shape=shapes,
        input_output_aliases=aliases,
        compiler_params=params(),
        cost_estimate=pl.CostEstimate(flops=8 * size, bytes_accessed=12 * size, transcendentals=0),
        name="update",
    )(*operands)


def update_in_parts(terms, owned):
    own, near, joined, direct_2, direct_3 = terms
    many, pix = owned.shape
    half, whole = (jax.ShapeDtypeStruct((many, size), jnp.bfloat16) for size in (pix // 2, pix))

    def second(own_ref, near_1_ref, direct_2_ref, direct_3_ref, owned_ref, *outs):
        dense_update_kernel((1,), own_ref, (None, near_1_ref), None, direct_2_ref, direct_3_ref, owned_ref, *outs)

    def first(own_ref, near_0_ref, near_1_ref, joined_ref, direct_2_ref, direct_3_ref, owned_ref, _, *outs):
        near_refs = (near_0_ref, near_1_ref)
        dense_update_kernel((0,), own_ref, near_refs, joined_ref, direct_2_ref, direct_3_ref, owned_ref, *outs)

    part_1, begun = update_call(second, (own, near[1], direct_2, direct_3, owned), [half, whole])
    operands = (own, *near, joined, direct_2, direct_3, owned, begun)
    part_0, done = update_call(first, operands, [half, whole], {7: 1})
    return [done, part_1, part_0]


def local(sizes, frames, slices, log_prior, orient):
    along, across = sizes
    owned, pix = slices.shape
    dense = along == 4 and owned == 4 and pix % 2048 == 0
    owned_b = round_slices(slices) if dense else [slices.astype(jnp.bfloat16)]
    if not dense:
        here, turned, prior = load_frames(frames, orient, log_prior, dense)
    for step in range(ITERS):
        last = step + 1 == ITERS
        if dense:
            blocks, over = gather_line(*owned_b)
            if step == 0:
                frames, over = lax.optimization_barrier((frames, over))
                here, turned, prior = load_frames(frames, orient, log_prior, dense)
            pieces = gathered_pieces(pix, step % 2)
        else:
            blocks = [lax.all_gather(owned_b[0], "frame", axis=0, tiled=True)]
            pieces = [(piece.start, piece.size, [(0, piece.start)]) for piece in chunks(pix, 512)]
        parts = exchange_all(
            score_parts(blocks, pieces, along * owned, turned), ("panel", "sub"), across
        )
        totals = block_totals(parts, prior, here, dense, not last)
        if dense:
            terms = scatter_line(*totals)
        else:
            whole = totals[0].reshape(along, owned, totals[0].shape[1])
            terms = [lax.all_to_all(whole, "frame", split_axis=0, concat_axis=0, tiled=False)]
        if dense and not last:
            owned_b = update_in_parts(terms, owned_b[0])
        else:
            kernel = last_update_kernel if dense else plain_update_kernel
            if dense:
                terms[1:2] = terms[1]
            shape = jax.ShapeDtypeStruct(slices.shape, jnp.float32 if last else jnp.bfloat16)
            owned_b = update_call(kernel, (*terms, owned_b[0]), [shape])
    return owned_b[0]


def solution(mesh):
    in_specs = (
        P(("groups", "frame"), ("panel", "sub")),
        P(("groups", "frame"), ("panel", "sub")),
        P(),
        P("groups"),
    )
    out_specs = P(("groups", "frame"), ("panel", "sub"))
    sizes = (mesh.shape["frame"], mesh.shape["panel"] * mesh.shape["sub"])
    return jax.shard_map(
        functools.partial(local, sizes), mesh=mesh, in_specs=in_specs, out_specs=out_specs, check_vma=False
    )
```

```python
import functools
import math

import jax
import jax.numpy as jnp
from jax import lax
from jax.experimental import pallas as pl
from jax.experimental.pallas import tpu as pltpu
from jax.sharding import PartitionSpec as P

PIX = 65536
ITERS = 2
LEAD = 1
TAIL = 128
VMEM_BYTES = 12 * 1024 * 1024
IN_VMEM = pl.BlockSpec(memory_space=pltpu.VMEM)


def params():
    return pltpu.CompilerParams(vmem_limit_bytes=VMEM_BYTES)


def tree_sum(terms):
    while len(terms) > 1:
        terms = [a + b for a, b in zip(terms[::2], terms[1::2])] + terms[len(terms) & ~1 :]
    return terms[0]


def chunks(size, most):
    step = math.gcd(size, most)
    return [pl.ds(at, step) for at in range(0, size, step)]


def rotate_rows(value, by):
    return value if by == 0 else jnp.concatenate([value[by:], value[:by]], axis=0)


def early(value, flops):
    return pl.pallas_call(
        lambda in_ref, out_ref: None,
        in_specs=[pl.BlockSpec(memory_space=pl.ANY)],
        out_specs=pl.BlockSpec(memory_space=pl.ANY),
        out_shape=jax.ShapeDtypeStruct(value.shape, value.dtype),
        input_output_aliases={0: 0},
        compiler_params=params(),
        cost_estimate=pl.CostEstimate(flops=flops, bytes_accessed=0, transcendentals=0),
        name="early",
    )(value)


def swap(value, distance):
    return lax.ppermute(value, "frame", [(i, i ^ distance) for i in range(4)])


def gather_line(whole, relayed, direct):
    over = swap(relayed, 2)
    direct_2 = swap(direct, 2)
    direct_3 = swap(direct, 3)
    near = swap(whole, 1)
    return [whole, near, over, direct_2, swap(over, 1), direct_3], over


def round_kernel(slices_ref, whole_ref, first_ref, second_ref, held_ref, sems):
    pix = slices_ref.shape[1]
    quarter, half = pix // 4, pix // 8
    copies = [
        pltpu.make_async_copy(
            slices_ref.at[:, pl.ds(q * quarter, quarter)], held_ref.at[:, pl.ds(q * quarter, quarter)], sems.at[q]
        )
        for q in range(4)
    ]
    for copy in copies:
        copy.start()
    for q, copy in enumerate(copies):
        copy.wait()
        for part, out_ref in enumerate((first_ref, second_ref)):
            there = pl.ds(q * quarter + part * half, half)
            value = held_ref[:, there].astype(jnp.bfloat16)
            whole_ref[:, there] = value
            out_ref[:, pl.ds(q * half, half)] = value


def round_slices(slices):
    owned, pix = slices.shape
    return pl.pallas_call(
        round_kernel,
        in_specs=[pl.BlockSpec(memory_space=pl.ANY)],
        out_specs=[IN_VMEM] * 3,
        out_shape=[jax.ShapeDtypeStruct((owned, size), jnp.bfloat16) for size in (pix, pix // 2, pix // 2)],
        scratch_shapes=[pltpu.VMEM((owned, pix), slices.dtype), pltpu.SemaphoreType.DMA((4,))],
        compiler_params=params(),
        cost_estimate=pl.CostEstimate(flops=5 * 10**9, bytes_accessed=8 * slices.size, transcendentals=0),
        name="round_slices",
    )(pltpu.with_memory_space_constraint(slices, pltpu.HBM))


def relay_kernel(came_ref, own_ref, out_ref):
    for piece in chunks(own_ref.shape[1], 512):
        came = rotate_rows(came_ref[:, piece].astype(jnp.float32), 4)
        out_ref[:, piece] = (came + own_ref[:, piece].astype(jnp.float32)).astype(jnp.bfloat16)


def scatter_line(own, *others):
    *near, relayed_2, direct_2, relayed_3, direct_3 = others
    came = swap(relayed_3, 1)
    joined = pl.pallas_call(
        relay_kernel,
        in_specs=[IN_VMEM] * 2,
        out_specs=IN_VMEM,
        out_shape=jax.ShapeDtypeStruct(came.shape, came.dtype),
        compiler_params=params(),
        cost_estimate=pl.CostEstimate(flops=2 * came.size, bytes_accessed=6 * came.size, transcendentals=0),
        name="relay",
    )(came, relayed_2)
    joined = swap(joined, 2)
    direct_3 = early(swap(direct_3, 3), 10**9)
    direct_2 = early(swap(direct_2, 2), 10**9)
    if len(near) > 1:
        direct_2, near_0 = lax.optimization_barrier((direct_2, near[0]))
        near = [swap(near_0, 1), swap(near[1], 1)]
    else:
        near = [swap(near[0], 1)]
    return [own, near, joined, direct_2, direct_3]


def exchange_all(part, axes, size):
    if size & (size - 1):
        return [lax.psum(part, axes)]
    return [part] + [lax.ppermute(part, axes, [(i, i ^ k) for i in range(size)]) for k in range(1, size)]


def load_kernel(dense, here_ref, orient_in_ref, log_prior_in_ref, turned_ref, prior_ref, orient_ref, log_prior_ref, sems):
    tables = [
        pltpu.make_async_copy(orient_in_ref, orient_ref, sems.at[0]),
        pltpu.make_async_copy(log_prior_in_ref, log_prior_ref, sems.at[1]),
    ]
    for copy in tables:
        copy.start()
    for piece in chunks(here_ref.shape[1], 512):
        turned_ref[piece, :] = here_ref[:, piece].T
    for table in tables:
        table.wait()
    many, columns = prior_ref.shape
    place = lax.axis_index("frame")
    for row in range(many):
        spot = 4 * (place ^ (row // 4)) + row % 4 if dense else row
        prior_ref[row : row + 1, :] = jnp.full((1, columns), log_prior_ref[orient_ref[spot]], jnp.float32)


def load_frames(frames, orient, log_prior, dense):
    rows, pix = frames.shape
    here = pltpu.with_memory_space_constraint(frames, pltpu.VMEM)
    turned, prior = pl.pallas_call(
        functools.partial(load_kernel, dense),
        in_specs=[IN_VMEM] + [pl.BlockSpec(memory_space=pl.ANY)] * 2,
        out_specs=[IN_VMEM] * 2,
        out_shape=[
            pltpu.VMEM((pix, rows), frames.dtype),
            jax.ShapeDtypeStruct((orient.shape[0], rows), jnp.float32),
        ],
        scratch_shapes=[
            pltpu.SMEM(orient.shape, orient.dtype),
            pltpu.SMEM(log_prior.shape, log_prior.dtype),
            pltpu.SemaphoreType.DMA((2,)),
        ],
        compiler_params=params(),
        cost_estimate=pl.CostEstimate(flops=0, bytes_accessed=6 * rows * pix, transcendentals=0),
        name="load_frames",
    )(here, *(pltpu.with_memory_space_constraint(x, pltpu.HBM) for x in (orient, log_prior)))
    return frames, turned, prior


def score_kernel(pieces, *refs):
    turned_ref, out_ref = refs[-2:]
    raw, squares = [], []
    for first, size, rows in pieces:
        model = jnp.concatenate([refs[ref][:, pl.ds(column, size)] for ref, column in rows], axis=0)
        raw.append(jnp.dot(model, turned_ref[pl.ds(first, size), :], preferred_element_type=jnp.float32))
        wide = model.astype(jnp.float32)
        squares.append(tree_sum([jnp.square(wide[:, at : at + 128]) for at in range(0, wide.shape[1], 128)]))
        if len(raw) > 4:
            raw, squares = raw[1:4] + [raw[0] + raw[4]], squares[1:4] + [squares[0] + squares[4]]
    out_ref[...] = tree_sum(raw) - 0.5 * jnp.sum(tree_sum(squares), axis=1, keepdims=True)


def score_parts(blocks, pieces, many, turned):
    pix, rows = turned.shape
    return pl.pallas_call(
        functools.partial(score_kernel, pieces),
        in_specs=[IN_VMEM] * (len(blocks) + 1),
        out_specs=IN_VMEM,
        out_shape=jax.ShapeDtypeStruct((many, rows), jnp.float32),
        compiler_params=params(),
        cost_estimate=pl.CostEstimate(flops=2 * rows * pix * many, bytes_accessed=2 * rows * pix, transcendentals=0),
        name="score_parts",
    )(*blocks, pltpu.with_memory_space_constraint(turned, pltpu.VMEM))


def gathered_pieces(pix, relayed):
    quarter = pix // 4
    half = quarter // 2
    pieces = []
    for part in range(2):
        for q in range(4):
            for at in range(0, half, math.gcd(half, 512)):
                there, here = q * quarter + part * half + at, q * half + at
                direct = part != relayed
                rows = [(0, there), (1, there), (2 + direct, here), (4 + direct, here)]
                pieces.append((there, math.gcd(half, 512), rows))
    return pieces


def split(counts):
    high = counts.astype(jnp.bfloat16).astype(jnp.float32)
    lane = lax.broadcasted_iota(jnp.int32, (counts.shape[0], TAIL), 1)
    return jnp.where(lane < TAIL // 2, high, counts - high)


def weigh(parts, prior_ref):
    raw = tree_sum([ref[...] for ref in parts])
    scores = (3.0 / math.sqrt(PIX)) * raw + prior_ref[...]
    up = jnp.exp(scores - jnp.max(scores, axis=0, keepdims=True))
    weights = (up / jnp.sum(up, axis=0, keepdims=True)).astype(jnp.bfloat16).astype(jnp.float32)
    counts = jnp.sum(weights, axis=1, keepdims=True)
    return weights, split(counts)


def plain_totals_kernel(n, *refs):
    parts, prior_ref, frames_ref, out_ref = refs[:n], refs[n], refs[n + 1], refs[n + 2]
    weights, tail = weigh(parts, prior_ref)
    weights = weights.astype(jnp.bfloat16)
    pix = frames_ref.shape[1]
    for piece in chunks(pix, 512):
        total = jnp.dot(weights, frames_ref[:, piece], preferred_element_type=jnp.float32)
        out_ref[:, piece] = total.astype(jnp.bfloat16)
    out_ref[:, pix:] = tail.astype(jnp.bfloat16)


def dense_totals_kernel(part, weights, frames_ref, own_ref, near_ref, two_ref, three_ref):
    quarter = frames_ref.shape[1] // 4
    half = quarter // 2
    turned = [rotate_rows(weights, (-4 * q) % 16).astype(jnp.bfloat16) for q in range(4)]
    for piece in chunks(half, 512):
        totals = [
            jnp.dot(
                turned[q],
                frames_ref[:, pl.ds(q * quarter + part * half + piece.start, piece.size)],
                preferred_element_type=jnp.float32,
            )
            for q in range(4)
        ]
        upper = lax.broadcasted_iota(jnp.int32, (8, piece.size), 0) < 4
        whole = pl.ds(part * half + piece.start, piece.size)
        near = whole if near_ref.shape[1] > quarter else piece
        spots = [(own_ref, whole), (near_ref, near), (two_ref, piece), (three_ref, piece)]
        for k, (out_ref, spot) in enumerate(spots):
            first = jnp.where(upper, totals[-k % 4][:8], totals[(1 - k) % 4][:8])
            second = jnp.where(upper, totals[(2 - k) % 4][8:], totals[(3 - k) % 4][8:])
            out_ref[:, spot] = jnp.concatenate([first, second], axis=0).astype(jnp.bfloat16)


def put_counts(tail, outs):
    for k, out_ref in outs:
        rows = jnp.concatenate([tail[4 * k : 4 * k + 4]] * 4, axis=0)
        out_ref[:, out_ref.shape[1] - TAIL :] = rows.astype(jnp.bfloat16)


def whole_totals_kernel(n, *refs):
    parts, prior_ref, frames_ref = refs[:n], refs[n], refs[n + 1]
    own_ref, near_0_ref, near_1_ref, two_0_ref, two_1_ref, three_0_ref, three_1_ref = refs[n + 2 :]
    weights, tail = weigh(parts, prior_ref)
    put_counts(tail, ((0, own_ref), (1, near_1_ref), (2, two_1_ref), (3, three_1_ref)))
    dense_totals_kernel(0, weights, frames_ref, own_ref, near_0_ref, two_0_ref, three_0_ref)
    dense_totals_kernel(1, weights, frames_ref, own_ref, near_1_ref, two_1_ref, three_1_ref)


def first_totals_kernel(n, part, *refs):
    parts, prior_ref, frames_ref, outs, weights_ref = refs[:n], refs[n], refs[n + 1], refs[n + 2 : n + 6], refs[n + 6]
    weights, tail = weigh(parts, prior_ref)
    weights_ref[...] = weights
    put_counts(tail, list(enumerate(outs)) if part else list(enumerate(outs[:2])))
    dense_totals_kernel(part, weights, frames_ref, *outs)


def second_totals_kernel(part, weights_ref, frames_ref, _own_ref, _near_ref, *outs):
    weights = weights_ref[...]
    if part:
        put_counts(split(jnp.sum(weights, axis=1, keepdims=True)), ((2, outs[2]), (3, outs[3])))
    dense_totals_kernel(part, weights, frames_ref, *outs)


def totals_call(kernel, operands, shapes, frames, aliases={}):
    rows, pix = frames.shape
    many = 16
    return pl.pallas_call(
        kernel,
        in_specs=[IN_VMEM] * len(operands),
        out_specs=[IN_VMEM] * len(shapes),
        out_shape=shapes,
        input_output_aliases=aliases,
        compiler_params=params(),
        cost_estimate=pl.CostEstimate(
            flops=rows * pix * many, bytes_accessed=rows * pix, transcendentals=rows * many
        ),
        name="block_totals",
    )(*operands)


def block_totals(parts, prior, frames, dense, near_halves):
    rows, pix = frames.shape
    many = prior.shape[0]
    frames = pltpu.with_memory_space_constraint(frames, pltpu.VMEM)
    if not dense:
        whole = jax.ShapeDtypeStruct((many, pix + TAIL), jnp.bfloat16)
        return totals_call(
            functools.partial(plain_totals_kernel, len(parts)), (*parts, prior, frames), [whole], frames
        )
    whole, half, half_tail = (
        jax.ShapeDtypeStruct((16, size), jnp.bfloat16) for size in (pix // 4 + TAIL, pix // 8, pix // 8 + TAIL)
    )
    if near_halves:
        return totals_call(
            functools.partial(whole_totals_kernel, len(parts)),
            (*parts, prior, frames),
            [whole, half, half_tail, half, half_tail, half, half_tail],
            frames,
        )
    sizes = (half, half_tail)
    own, near, two, three, weights = totals_call(
        functools.partial(first_totals_kernel, len(parts), LEAD),
        (*parts, prior, frames),
        [whole, whole, sizes[LEAD], sizes[LEAD], jax.ShapeDtypeStruct((many, rows), jnp.float32)],
        frames,
    )
    own, near, *other = totals_call(
        functools.partial(second_totals_kernel, 1 - LEAD),
        (weights, frames, own, near),
        [whole, whole, sizes[1 - LEAD], sizes[1 - LEAD]],
        frames,
        {2: 0, 3: 1},
    )
    twos, threes = (two, other[0]), (three, other[1])
    return own, near, twos[LEAD], twos[1 - LEAD], threes[LEAD], threes[1 - LEAD]


def plain_update_kernel(terms_ref, owned_ref, out_ref):
    pix = owned_ref.shape[1]
    tail = jnp.sum(terms_ref[:, :, pix:].astype(jnp.float32), axis=0)
    counts = tail[:, :1] + tail[:, TAIL // 2 : TAIL // 2 + 1]
    for piece in chunks(pix, 512):
        total = jnp.sum(terms_ref[:, :, piece].astype(jnp.float32), axis=0)
        out_ref[:, piece] = ((total + owned_ref[:, piece].astype(jnp.float32)) / (counts + 1.0)).astype(out_ref.dtype)


def dense_update_kernel(parts, *refs):
    own_ref, near_refs, joined_ref, direct_2_ref, direct_3_ref, owned_ref = refs[:6]
    out_ref, half_refs = refs[-1], refs[-2:-1]
    if len(refs) < 8:
        half_refs = []
    quarter = owned_ref.shape[1] // 4
    half = quarter // 2

    def total(terms):
        return tree_sum([rotate_rows(ref[:, spot].astype(jnp.float32), 4 * k) for k, ref, spot in terms])

    behind, behind_half = pl.ds(quarter, TAIL), pl.ds(half, TAIL)
    tail = total(
        [
            (0, own_ref, behind),
            (1, near_refs[-1], behind_half if len(near_refs) > 1 else behind),
            (2, direct_2_ref, behind_half),
            (3, direct_3_ref, behind_half),
        ]
    )
    scale = 1.0 / (tail[:, :1] + tail[:, TAIL // 2 : TAIL // 2 + 1] + 1.0)
    for part in parts:
        for piece in chunks(half, 512):
            whole = pl.ds(part * half + piece.start, piece.size)
            terms = [(0, own_ref, whole)]
            terms += [(1, near_refs[part], piece) if len(near_refs) > 1 else (1, near_refs[0], whole)]
            terms += [(2, direct_2_ref, piece), (3, direct_3_ref, piece)] if part else [(2, joined_ref, piece)]
            spots = [pl.ds(q * quarter + whole.start, whole.size) for q in range(4)]
            owned = jnp.concatenate([owned_ref[:, spot].astype(jnp.float32) for spot in spots], axis=0)
            new = ((total(terms) + owned) * scale).astype(out_ref.dtype)
            for q, spot in enumerate(spots):
                out_ref[:, spot] = new[4 * q : 4 * q + 4]
                for half_ref in half_refs:
                    half_ref[:, pl.ds(q * half + piece.start, piece.size)] = new[4 * q : 4 * q + 4]


def last_update_kernel(own_ref, near_ref, *refs):
    dense_update_kernel((0, 1), own_ref, (near_ref,), *refs)


def update_call(kernel, operands, shapes, aliases={}):
    size = operands[0].size
    return pl.pallas_call(
        kernel,
        in_specs=[IN_VMEM] * len(operands),
        out_specs=[IN_VMEM] * len(shapes),
        out_shape=shapes,
        input_output_aliases=aliases,
        compiler_params=params(),
        cost_estimate=pl.CostEstimate(flops=8 * size, bytes_accessed=12 * size, transcendentals=0),
        name="update",
    )(*operands)


def update_in_parts(terms, owned):
    own, near, joined, direct_2, direct_3 = terms
    many, pix = owned.shape
    half, whole = (jax.ShapeDtypeStruct((many, size), jnp.bfloat16) for size in (pix // 2, pix))

    def second(own_ref, near_1_ref, direct_2_ref, direct_3_ref, owned_ref, *outs):
        dense_update_kernel((1,), own_ref, (None, near_1_ref), None, direct_2_ref, direct_3_ref, owned_ref, *outs)

    def first(own_ref, near_0_ref, near_1_ref, joined_ref, direct_2_ref, direct_3_ref, owned_ref, _, *outs):
        near_refs = (near_0_ref, near_1_ref)
        dense_update_kernel((0,), own_ref, near_refs, joined_ref, direct_2_ref, direct_3_ref, owned_ref, *outs)

    part_1, begun = update_call(second, (own, near[1], direct_2, direct_3, owned), [half, whole])
    operands = (own, *near, joined, direct_2, direct_3, owned, begun)
    part_0, done = update_call(first, operands, [half, whole], {7: 1})
    return [done, part_1, part_0]


def local(sizes, frames, slices, log_prior, orient):
    along, across = sizes
    owned, pix = slices.shape
    dense = along == 4 and owned == 4 and pix % 2048 == 0
    owned_b = round_slices(slices) if dense else [slices.astype(jnp.bfloat16)]
    if not dense:
        here, turned, prior = load_frames(frames, orient, log_prior, dense)
    for step in range(ITERS):
        last = step + 1 == ITERS
        if dense:
            blocks, over = gather_line(*owned_b)
            if step == 0:
                frames, over = lax.optimization_barrier((frames, over))
                here, turned, prior = load_frames(frames, orient, log_prior, dense)
            pieces = gathered_pieces(pix, step % 2)
        else:
            blocks = [lax.all_gather(owned_b[0], "frame", axis=0, tiled=True)]
            pieces = [(piece.start, piece.size, [(0, piece.start)]) for piece in chunks(pix, 512)]
        parts = exchange_all(
            score_parts(blocks, pieces, along * owned, turned), ("panel", "sub"), across
        )
        totals = block_totals(parts, prior, here, dense, not last)
        if dense:
            terms = scatter_line(*totals)
        else:
            whole = totals[0].reshape(along, owned, totals[0].shape[1])
            terms = [lax.all_to_all(whole, "frame", split_axis=0, concat_axis=0, tiled=False)]
        if dense and not last:
            owned_b = update_in_parts(terms, owned_b[0])
        else:
            kernel = last_update_kernel if dense else plain_update_kernel
            if dense:
                terms[1:2] = terms[1]
            shape = jax.ShapeDtypeStruct(slices.shape, jnp.float32 if last else jnp.bfloat16)
            owned_b = update_call(kernel, (*terms, owned_b[0]), [shape])
    return owned_b[0]


def solution(mesh):
    in_specs = (
        P(("groups", "frame"), ("panel", "sub")),
        P(("groups", "frame"), ("panel", "sub")),
        P(),
        P("groups"),
    )
    out_specs = P(("groups", "frame"), ("panel", "sub"))
    sizes = (mesh.shape["frame"], mesh.shape["panel"] * mesh.shape["sub"])
    return jax.shard_map(
        functools.partial(local, sizes), mesh=mesh, in_specs=in_specs, out_specs=out_specs, check_vma=False
    )
```
